32 devices in a mesh: ed: 8 (over z, core), ep: 4 (over y, x).
Axes of the slice: x: 2, y: 2, z: 4, core: 2. Of those that a mesh axis runs over, the one named last changes fastest.
Arguments:
- out_grad: bfloat16 [4096, 3584], P(('ed', 'ep')), may hold values from -4.1 to 4.1
- routes: int32 [4096, 2], P(('ed', 'ep')), may hold values from 0 to 3, all different within a row; in each aligned block of 128 rows (0 to 127, 128 to 255, ...) at most 128 rows name the same one
- gates: bfloat16 [4096, 2], P(('ed', 'ep')), may hold values from 0.049804688 to 0.59765625
- pre_acts: bfloat16 [8, 4, 4, 128, 2048], P('ed', 'ep'), may hold values from -6 to 6
- down_weight: bfloat16 [4, 1024, 3584], P('ep'), may hold values from -0.1875 to 0.1875
- history: float32 [8, 4, 16], P('ed', 'ep'), may hold values from 4 to 32
Outputs:
- pre_grad: bfloat16 [8, 4, 4, 128, 2048], P('ed', 'ep')
- wgrad: float32 [4, 3584, 1024], P('ep', 'ed')
- new_history: float32 [4, 16], P('ep')
- gate_grad: float32 [4096, 2], P(('ed', 'ep'))
The draws below stay inside these ranges and needn't reach their ends.
Inputs may be any that keep to these rules, and one draw needn't show every extreme that they name: `routes`: each token names 2 different experts; among the 128 rows of one device no expert is named more than 128 times, and in some device's rows one expert is named exactly 128 times.
All inputs are finite; a program needn't handle non-finite values.
Results may differ from the reference program's by a relative error of at most 0.025.
Values may be sent and summed in bfloat16 or wider, within the bound.
A program may use at most 128 MiB of HBM per device.

```python
import math
import jax
import jax.numpy as jnp
import numpy as np
from jax import lax

D = 3584
EXPERT_FF = 1024
TOPW = 2
HIST = 16
TOK_DEV = 128
EXPERTS = 4
CAP = 128
TOKENS = 4096
N_ED = 8
N_EP = 4


def draw_out_grad(key, part):
    key = jax.random.fold_in(key, 7)
    first, second = jax.random.split(key, 2)
    column = jnp.arange(D, dtype=jnp.float32) / max(D - 1, 1)
    rough = jnp.exp(jax.random.uniform(second, (D,), jnp.float32, -0.4, 0.4))
    column_scale = 0.1 * jnp.exp(1.5 * column) * rough
    base = jnp.clip(jax.random.normal(first, (TOKENS, D), jnp.float32), -6.0, 6.0)
    values = base * column_scale[None, :]
    return values.astype(jnp.bfloat16)


def block_levels(stream_key, shape, shards, low, top_value):
    def one(axis_at, blocks):
        heights = jax.random.uniform(jax.random.fold_in(jax.random.fold_in(stream_key, 6), axis_at), (blocks,), jnp.float32, low / len(shards), top_value / len(shards))
        return jnp.repeat(jnp.exp(heights), shape[axis_at] // blocks).reshape((-1,) + (1,) * (len(shape) - axis_at - 1))

    gain = one(*shards[0])
    for cut in shards[1:]:
        gain = gain * one(*cut)
    return gain


def assign_block(key, own, number, rows, count, top, bound, skew):
    ranking = jax.random.permutation(key, count)
    heavy_load, usual = portions_of(count, rows * top, bound, skew, True), portions_of(count, rows * top, bound, skew, False)
    places = jnp.arange(count)

    def named(lengths, offset_by):
        used = int((lengths > 0).sum())
        fixed = max(1, used // 4)
        moved = fixed + (places - fixed + offset_by * (used - fixed)) % max(1, count - fixed)
        return jnp.zeros((count,), jnp.int32).at[ranking[jnp.where(places < fixed, places, moved)]].set(jnp.asarray(lengths, jnp.int32))

    lengths = jnp.where(number % 4 == 0, named(heavy_load, number // 4), named(usual, number - number // 4 - 1))
    mixed = jax.random.permutation(jax.random.fold_in(own, 3), count)
    giver, sink = mixed[0:count // 2 * 2:2], mixed[1:count // 2 * 2:2]
    room = jnp.minimum(lengths[giver] - 1, bound - lengths[sink]) // 2
    room = jnp.where((giver == ranking[0]) | (sink == ranking[0]) | (lengths[sink] == 0), 0, jnp.maximum(room, 0))
    moved = jax.random.randint(jax.random.fold_in(own, 4), (count // 2,), 0, 1 << 20) % (room + 1)
    lengths = lengths.at[giver].add(-moved).at[sink].add(moved)
    labels = jnp.searchsorted(jnp.cumsum(lengths), jnp.arange(rows * top), side="right").astype(jnp.int32)
    listing = labels.reshape(top, rows).T
    listing = listing[jax.random.permutation(jax.random.fold_in(own, 1), rows)]
    offset_by = jax.random.randint(jax.random.fold_in(own, 2), (rows, 1), 0, top)
    return jnp.take_along_axis(listing, (jnp.arange(top)[None, :] + offset_by) % top, axis=1)


def portions_of(number_of, total, most, skew, full):
    portions = [(1 << 20) // math.isqrt(standing ** skew) + 1 for standing in range(1, number_of + 1)]
    largest = most if full else min(most, max(-(-total // number_of), total * portions[0] // sum(portions)))
    least = 1 if total - largest >= number_of - 1 else 0
    given, surplus = [largest] + [least] * (number_of - 1), total - largest - least * (number_of - 1)
    while surplus > 0:
        free = [i for i in range(1, number_of) if given[i] < largest] or [i for i in range(1, number_of) if given[i] < most]
        pool, budget = sum([portions[i] for i in free]), surplus
        for i in free:
            addition = min(most - given[i], max(1, budget * portions[i] // pool), surplus)
            given[i] = given[i] + addition
            surplus = surplus - addition
    return np.array(given)


def noise(stream_key, shape, scale, limit, shards=(), held_as=jnp.bfloat16):
    level = block_levels(stream_key, shape, shards, -0.22, 0.18) if shards else 1.0
    entries = jax.random.normal(stream_key, shape, jnp.float32) * scale * level
    return jnp.minimum(jnp.maximum(entries, -limit), limit).astype(held_as)


def setup_inputs(seed: int = 0) -> dict:
    arg_keys = jax.random.split(jax.random.key(seed), 7)
    out_grad = draw_out_grad(jax.random.fold_in(arg_keys[6], 71), 0)
    routes_keys = jax.random.split(jax.random.fold_in(arg_keys[1], 1), TOKENS // TOK_DEV)
    routes_turns = jax.random.permutation(jax.random.fold_in(arg_keys[1], 3), TOKENS // TOK_DEV)
    routes = jax.vmap(lambda own, number: assign_block(jax.random.fold_in(arg_keys[1], 2), own, number, TOK_DEV, EXPERTS, TOPW, CAP, 2))(routes_keys, routes_turns).reshape((TOKENS, TOPW))
    gates = jnp.clip(0.049804688 + 0.54785156 * jax.random.uniform(arg_keys[2], (TOKENS, TOPW), jnp.float32) ** block_levels(arg_keys[2], (TOKENS, TOPW), ((0, 32),), -0.2, 0.2), 0.049804688, 0.59765625).astype(jnp.bfloat16)
    pre_acts = noise(arg_keys[3], (N_ED, EXPERTS, N_EP, CAP, 2 * EXPERT_FF), 1.0, 6.0, ((0, 8), (1, 4)))
    down_weight = noise(arg_keys[4], (EXPERTS, EXPERT_FF, D), EXPERT_FF ** -0.5, 0.1875, ((0, 4),))
    history = jnp.clip(jnp.exp(math.log(32.0) - 2.0794415 * jax.random.uniform(arg_keys[5], (N_ED, EXPERTS, HIST), jnp.float32) ** block_levels(arg_keys[5], (N_ED, EXPERTS, HIST), ((0, 8), (1, 4)), -0.2, 0.2)), 4.0, 32.0)
    return dict(out_grad=out_grad, routes=routes, gates=gates, pre_acts=pre_acts, down_weight=down_weight, history=history)


def route_slots(routes):
    flat = routes.reshape(N_ED * N_EP, TOK_DEV * TOPW)
    hits = (flat[:, :, None] == jnp.arange(EXPERTS, dtype=jnp.int32)[None, None, :]).astype(jnp.int32)
    before = jnp.cumsum(hits, axis=1) - hits
    return jnp.sum(before * hits, axis=2).reshape(TOKENS, TOPW)


def reference(out_grad, routes, gates, pre_acts, down_weight, history):
    slot = route_slots(routes)
    block = (jnp.arange(TOKENS, dtype=jnp.int32) // TOK_DEV)[:, None]
    replica = block // N_EP
    source = block % N_EP
    target = ((((replica * EXPERTS + routes) * N_EP + source) * CAP) + slot).reshape(-1).astype(jnp.int32)
    total = N_ED * EXPERTS * N_EP * CAP
    owner = jnp.arange(TOKENS * TOPW, dtype=jnp.int32) // TOPW
    table = jnp.zeros((total,), jnp.int32).at[target].set(owner + 1)
    picked = out_grad[jnp.maximum(table - 1, 0)]
    rows_all = jnp.where((table > 0)[:, None], picked, jnp.zeros_like(picked))
    rows_all = rows_all.reshape(N_ED, EXPERTS, N_EP * CAP, D)
    gate_all = jnp.zeros((total,), jnp.bfloat16).at[target].set(gates.reshape(-1))
    gate_all = gate_all.reshape(N_ED, EXPERTS, N_EP * CAP)
    pre_all = pre_acts.reshape(N_ED, EXPERTS, N_EP * CAP, 2 * EXPERT_FF)
    merged = jnp.max(history, axis=0)
    ref_amax = jnp.max(merged, axis=1)
    scale = 1.0 / ref_amax

    def per_expert(expert):
        weight = down_weight[expert]
        factor = scale[expert]

        def step(accum, rep):
            rows_in = rows_all[rep, expert]
            gate_row = gate_all[rep, expert].astype(jnp.float32)[:, None]
            pre_block = pre_all[rep, expert]
            gate_pre = pre_block[:, :EXPERT_FF].astype(jnp.float32)
            up_pre = pre_block[:, EXPERT_FF:].astype(jnp.float32)
            sigma = jax.nn.sigmoid(gate_pre)
            act = (gate_pre * sigma * up_pre).astype(jnp.bfloat16)
            weighted = (gate_row * act.astype(jnp.float32)).astype(jnp.bfloat16)
            raw = jnp.dot(rows_in, weight.T, preferred_element_type=jnp.float32)
            score = jnp.sum(act.astype(jnp.float32) * raw, axis=1)
            grad_act = gate_row * raw
            grad_gate = grad_act * up_pre * sigma * (1.0 + gate_pre * (1.0 - sigma))
            grad_up = grad_act * gate_pre * sigma
            grad_pre = jnp.concatenate([grad_gate, grad_up], axis=1).astype(jnp.bfloat16)
            term = jnp.dot(rows_in.T, weighted, preferred_element_type=jnp.float32)
            part = (factor * term).astype(jnp.bfloat16)
            part = lax.optimization_barrier(part)
            return accum + part.astype(jnp.float32), (grad_pre, score)

        accum, (grad_pre, score) = lax.scan(step, jnp.zeros((D, EXPERT_FF), jnp.float32), jnp.arange(N_ED, dtype=jnp.int32))
        return accum, grad_pre, score

    wgrad, grad_pre, score = lax.map(per_expert, jnp.arange(EXPERTS, dtype=jnp.int32))
    pre_grad = jnp.transpose(grad_pre, (1, 0, 2, 3)).reshape(N_ED, EXPERTS, N_EP, CAP, 2 * EXPERT_FF)
    new_amax = jnp.max(jnp.abs(wgrad), axis=(1, 2)) * ref_amax
    new_history = jnp.concatenate([merged[:, 1:], new_amax[:, None]], axis=1)
    score_flat = jnp.transpose(score, (1, 0, 2)).reshape(-1)
    gate_grad = score_flat[target].reshape(TOKENS, TOPW)
    return pre_grad, wgrad, new_history, gate_grad
```

```python
import functools

import jax
import jax.numpy as jnp
from jax import lax
from jax.experimental import pallas as pl
from jax.experimental.pallas import tpu as pltpu
from jax.sharding import PartitionSpec as P


def split_pre(pre_block, width_ff):
    gate_pre = pre_block[:, :width_ff].astype(jnp.float32)
    up_pre = pre_block[:, width_ff:].astype(jnp.float32)
    return (gate_pre, up_pre, jax.nn.sigmoid(gate_pre))


def plain(out_grad, routes, gates, pre_acts, down_weight, history):
    tok_rows, top = routes.shape
    width = out_grad.shape[1]
    local = down_weight.shape[0]
    width_ff = down_weight.shape[1]
    n_src = pre_acts.shape[2]
    cap = pre_acts.shape[3]
    n_ep = lax.axis_size("ep")
    n_replicas = lax.axis_size("ed")
    experts = local * n_ep
    flat = routes.reshape(-1)
    hits = (flat[:, None] == jnp.arange(experts, dtype=jnp.int32)[None, :]).astype(jnp.int32)
    before = jnp.cumsum(hits, axis=0) - hits
    slot = jnp.sum(before * hits, axis=1)
    target = flat * cap + slot
    owner = jnp.arange(tok_rows * top, dtype=jnp.int32) // top
    table = jnp.zeros((experts * cap,), jnp.int32).at[target].set(owner + 1)
    picked = out_grad[jnp.maximum(table - 1, 0)]
    send_rows = jnp.where((table > 0)[:, None], picked, jnp.zeros_like(picked))
    send_gate = jnp.zeros((experts * cap,), jnp.bfloat16).at[target].set(gates.reshape(-1))
    arrived, arrived_gate = (
        lax.all_to_all(
            send_rows.reshape(n_ep, local * cap, width),
            "ep",
            split_axis=0,
            concat_axis=0,
            tiled=True,
        ),
        lax.all_to_all(
            send_gate.reshape(n_ep, local * cap), "ep", split_axis=0, concat_axis=0, tiled=True
        ),
    )
    arrived = (
        arrived.reshape(n_ep, local, cap, width)
        .transpose(1, 0, 2, 3)
        .reshape(local, n_ep * cap, width)
    )
    arrived_gate = (
        arrived_gate.reshape(n_ep, local, cap)
        .transpose(1, 0, 2)
        .reshape(local, n_ep * cap)
        .astype(jnp.float32)
    )
    merged = lax.pmax(history, "ed")[0]
    ref_amax = jnp.max(merged, axis=1)
    scale = 1.0 / ref_amax
    rows = arrived[0]
    gate_row = arrived_gate[0][:, None]
    weight = down_weight[0]
    pre_block = pre_acts[0, 0].reshape(n_src * cap, 2 * width_ff)
    gate_pre, up_pre, sigma = split_pre(pre_block, width_ff)
    act = (gate_pre * sigma * up_pre).astype(jnp.bfloat16)
    weighted = (gate_row * act.astype(jnp.float32)).astype(jnp.bfloat16)
    raw = jnp.einsum("rd,hd->rh", rows, weight, preferred_element_type=jnp.float32)
    score = jnp.sum(act.astype(jnp.float32) * raw, axis=1)
    grad_act = gate_row * raw
    grad_gate = grad_act * up_pre * sigma * (1.0 + gate_pre * (1.0 - sigma))
    grad_up = grad_act * gate_pre * sigma
    grads_pre = [
        jnp.concatenate([grad_gate, grad_up], axis=1)
        .astype(jnp.bfloat16)
        .reshape(n_src, cap, 2 * width_ff)
    ]
    scores = [score.reshape(n_ep, cap)]
    factor = scale[0]

    def term(start, count, rows=rows, weighted=weighted, factor=factor):
        return factor * jnp.einsum("rd,rh->dh", rows, weighted, preferred_element_type=jnp.float32)

    shard = lax.psum_scatter(
        term(jnp.int32(0), width // n_replicas * lax.axis_size("ed")).astype(jnp.bfloat16),
        "ed",
        scatter_dimension=0,
        tiled=True,
    ).astype(jnp.float32)
    shards = [shard]
    wgrad = jnp.stack(shards)
    peak = lax.pmax(jnp.max(jnp.abs(wgrad), axis=(1, 2)), "ed")
    new_amax = peak * ref_amax
    new_history = jnp.concatenate([merged[:, 1:], new_amax[:, None]], axis=1)
    pre_grad = jnp.stack(grads_pre)[None]
    outgoing = jnp.stack(scores).transpose(1, 0, 2).reshape(n_ep, local * cap)
    returned = lax.all_to_all(outgoing, "ep", split_axis=0, concat_axis=0, tiled=True)
    gate_grad = returned.reshape(-1)[target].reshape(tok_rows, top)
    return (pre_grad, wgrad, new_history, gate_grad)


MESH = pl.DeviceIdType.MESH
LANES = 128


def orders(n_z):
    centre = (n_z - 1) / 2
    return [
        sorted(range(n_z), key=lambda j: (-abs(j - z), -abs(j - centre), j)) for z in range(n_z)
    ]


def kernel(
    n_z,
    n_ep,
    cap,
    routes_ref,
    gates_ref,
    hist_ref,
    tok_hbm,
    pre_hbm,
    w_hbm,
    pg_hbm,
    wg_hbm,
    hist_out,
    gg_out,
    tok,
    wv,
    pre,
    pgrad,
    perm,
    perm_t,
    outrows,
    rows,
    sib,
    w2,
    raw,
    act,
    rt,
    acc,
    recv,
    zsend,
    gate_out,
    gate_in,
    score_out,
    score_in,
    hist_mine,
    hist_all,
    amax_mine,
    amax_all,
    tok_sem,
    w_sem,
    pre_sem,
    pg_sem,
    wg_sem,
    row_ss,
    row_rs,
    gate_ss,
    gate_rs,
    score_ss,
    score_rs,
    sib_ss,
    sib_rs,
    w2_ss,
    w2_rs,
    z_ss,
    z_rs,
    hist_ss,
    hist_rs,
    amax_ss,
    amax_rs,
):
    f32, bf16 = jnp.float32, jnp.bfloat16
    ed, me = lax.axis_index("ed"), lax.axis_index("ep")
    z, core = ed // 2, ed % 2
    n_ed = 2 * n_z
    sibling = z * 2 + 1 - core
    blk = tok.shape[2]
    half = blk // 2
    lane0 = half // LANES * LANES
    wid = blk - lane0
    sub = half // 2
    slots = n_ep * cap
    ff = act.shape[1]
    table = orders(n_z)

    def shard_at(i):
        j = jnp.int32(table[0][i])
        for at in range(1, n_z):
            j = jnp.where(z == at, jnp.int32(table[at][i]), j)
        return j

    shard = [shard_at(i) for i in range(n_z)]

    def columns(i):
        return pl.ds(pl.multiple_of(shard[i] * blk, LANES), blk)

    tok_in = [
        pltpu.make_async_copy(tok_hbm.at[:, columns(i)], tok.at[i], tok_sem.at[i])
        for i in range(n_z)
    ]
    w_in = [
        pltpu.make_async_copy(w_hbm.at[0, :, columns(i)], wv.at[i], w_sem.at[i])
        for i in range(n_z)
    ]
    pre_in = pltpu.make_async_copy(pre_hbm, pre, pre_sem.at[0])
    tok_in[0].start()
    pre_in.start()
    for i in range(1, n_z):
        tok_in[i].start()
    for i in range(n_z):
        w_in[i].start()

    barrier = pltpu.get_barrier_semaphore()
    for d in range(1, n_ep):
        pl.semaphore_signal(
            barrier, inc=1, device_id={"ep": lax.rem(me + d, n_ep)}, device_id_type=MESH
        )
    for d in range(1, n_ed):
        pl.semaphore_signal(
            barrier, inc=1, device_id={"ed": lax.rem(ed + d, n_ed)}, device_id_type=MESH
        )

    hist_mine[...] = jnp.zeros_like(hist_mine)
    hist_mine[0:1, 0 : hist_ref.shape[1]] = hist_ref[...]

    tokens = tok.shape[1]
    expert = lax.broadcasted_iota(jnp.int32, (tokens, slots), 1) // cap
    place = lax.broadcasted_iota(jnp.int32, (tokens, slots), 1) % cap
    hit0 = routes_ref[:, 0:1] == expert
    hit1 = routes_ref[:, 1:2] == expert
    hits = jnp.where(hit0, 1.0, 0.0) + jnp.where(hit1, 1.0, 0.0)
    earlier = lax.broadcasted_iota(jnp.int32, (tokens, tokens), 0) > lax.broadcasted_iota(
        jnp.int32, (tokens, tokens), 1
    )
    slot = jnp.dot(
        jnp.where(earlier, 1.0, 0.0).astype(bf16), hits.astype(bf16), preferred_element_type=f32
    )
    placed = jnp.where(slot == place.astype(f32), hits, 0.0)
    perm_t[...] = placed
    g0 = gates_ref[:, 0:1].astype(f32)
    g1 = gates_ref[:, 1:2].astype(f32)
    gate_tok = (jnp.where(hit0, g0, 0.0) + jnp.where(hit1, g1, 0.0)).astype(bf16)
    for e in range(n_ep):
        own = placed[:, e * cap : (e + 1) * cap].T.astype(bf16)
        perm[e] = own
        gate_out[e] = jnp.dot(
            own, gate_tok[:, e * cap : (e + 1) * cap], preferred_element_type=f32
        ).astype(bf16)
    gate_in[me] = gate_out[me]

    pl.semaphore_wait(barrier, n_ep - 1 + n_ed - 1)

    def to_ep(src, dst, ss, rs, d):
        return pltpu.make_async_remote_copy(
            src_ref=src, dst_ref=dst, send_sem=ss, recv_sem=rs,
            device_id={"ep": lax.rem(me + d, n_ep)}, device_id_type=MESH,
        )

    def to_ed(src, dst, ss, rs, target):
        return pltpu.make_async_remote_copy(
            src_ref=src, dst_ref=dst, send_sem=ss, recv_sem=rs,
            device_id={"ed": target}, device_id_type=MESH,
        )

    def peer(d):
        return lax.rem(me + d, n_ep)

    def row_copy(i, d, src):
        return to_ep(
            outrows.at[i, peer(d)], rows.at[i, src], row_ss.at[i, d], row_rs.at[i, src], d
        )

    def gate_copy(d, src):
        return to_ep(gate_out.at[peer(d)], gate_in.at[src], gate_ss.at[d], gate_rs.at[src], d)

    def score_copy(d, src):
        return to_ep(score_out.at[peer(d)], score_in.at[src], score_ss.at[d], score_rs.at[src], d)

    def hist_copy(d, src):
        return to_ed(
            hist_mine, hist_all.at[src], hist_ss.at[d], hist_rs.at[src], lax.rem(ed + d, n_ed)
        )

    def amax_copy(d, src):
        return to_ed(
            amax_mine, amax_all.at[src], amax_ss.at[d], amax_rs.at[src], lax.rem(ed + d, n_ed)
        )

    def dispatch(i):
        tok_in[i].wait()

        @pl.loop(0, n_ep)
        def _(e):
            outrows[i, e] = jnp.dot(perm[e], tok[i], preferred_element_type=f32).astype(bf16)

        for d in range(1, n_ep):
            row_copy(i, d, me).start()
        rows[i, me] = outrows[i, me]

    for d in range(1, n_ep):
        gate_copy(d, me).start()
    dispatch(0)
    for d in range(1, n_ed):
        hist_copy(d, ed).start()
    hist_all[ed] = hist_mine[...]

    tile = 32
    pre_in.wait()
    for d in range(1, n_ep):
        gate_copy(d, peer(d)).wait_recv()

    @pl.loop(0, slots // tile)
    def _(t):
        at = pl.ds(pl.multiple_of(t * tile, tile), tile)
        src, off = t // (cap // tile), t % (cap // tile)
        off = pl.multiple_of(off * tile, tile)
        g = pre[src, pl.ds(off, tile), 0:ff].astype(f32)
        u = pre[src, pl.ds(off, tile), ff:].astype(f32)
        a = (g * jax.nn.sigmoid(g) * u).astype(bf16)
        act[at, :] = a
        gate = gate_in[src, pl.ds(off, tile), 0:1].astype(f32)
        w2[core, at, :] = (gate * a.astype(f32)).astype(bf16)

    def w2_copy(which):
        return to_ed(w2.at[which], w2.at[which], w2_ss.at[0], w2_rs.at[0], sibling)

    w2_copy(core).start()

    def sib_copy(i):
        at = pl.ds(pl.multiple_of(lane0 * (1 - core), LANES), wid)
        return to_ed(rows.at[i, :, :, at], sib.at[i], sib_ss.at[i], sib_rs.at[i], sibling)

    def z_copy(i, s):
        right = shard[i] > z
        target = jnp.where(right, z + 1, z - 1)
        way = jnp.where(right, 0, 1)
        return to_ed(
            zsend.at[i, s], recv.at[way, shard[i], s], z_ss.at[i, s],
            z_rs.at[way, shard[i], s], target * 2 + core,
        )

    def z_arrival(way, j, s):
        return to_ed(
            zsend.at[0, 0], recv.at[way, j, s], z_ss.at[0, 0], z_rs.at[way, j, s], sibling
        )

    n_tile = 256
    etile = 32

    for i in range(n_z):
        last = i == n_z - 1
        for d in range(1, n_ep):
            row_copy(i, d, peer(d)).wait_recv()
        sib_copy(i).start()
        if not last:
            dispatch(i + 1)
        w_in[i].wait()

        @pl.loop(0, ff // n_tile)
        def _(n):
            at = pl.ds(pl.multiple_of(n * n_tile, n_tile), n_tile)
            got = lax.dot_general(
                rows[i].reshape(slots, blk), wv[i, at, :], (((1,), (1,)), ((), ())),
                preferred_element_type=f32,
            )
            if i == 0:
                raw[:, at] = got
            else:
                raw[:, at] += got

        if i == 0:
            w2_copy(1 - core).wait_recv()
        sib_copy(i).wait_recv()
        mine = pl.ds(pl.multiple_of(lane0 * core, LANES), wid)
        rt[:, pl.ds(pl.multiple_of(core * slots, LANES), slots)] = (
            rows[i, :, :, mine].reshape(slots, wid).T
        )
        rt[:, pl.ds(pl.multiple_of((1 - core) * slots, LANES), slots)] = (
            sib[i].reshape(slots, wid).T
        )
        start = pl.multiple_of((half - lane0) * core, 16)

        @pl.loop(0, ff // n_tile)
        def _(n):
            at = pl.ds(pl.multiple_of(n * n_tile, n_tile), n_tile)
            acc[:, at] = jnp.dot(
                rt[pl.ds(start, half), :],
                w2[:, :, at].reshape(2 * slots, n_tile),
                preferred_element_type=f32,
            )

        if last:
            break
        right = shard[i] > z
        way = jnp.where(right, 0, 1)
        fed = jnp.where(right, z > 0, z < n_z - 1)
        for s in range(2):

            @pl.when(fed)
            def _():
                z_arrival(way, shard[i], s).wait_recv()

                @pl.loop(0, sub // etile)
                def _(t):
                    off = pl.multiple_of(t * etile, etile)
                    own = acc[pl.ds(s * sub + off, etile), :]
                    came = recv[way, shard[i], s, pl.ds(off, etile), :].astype(f32)
                    zsend[i, s, pl.ds(off, etile), :] = (own + came).astype(bf16)

            @pl.when(jnp.logical_not(fed))
            def _():
                @pl.loop(0, sub // etile)
                def _(t):
                    off = pl.multiple_of(t * etile, etile)
                    own = acc[pl.ds(s * sub + off, etile), :]
                    zsend[i, s, pl.ds(off, etile), :] = own.astype(bf16)

            z_copy(i, s).start()

    @pl.loop(0, slots // tile)
    def _(t):
        at = pl.ds(pl.multiple_of(t * tile, tile), tile)
        src, off = t // (cap // tile), t % (cap // tile)
        off = pl.multiple_of(off * tile, tile)
        g = pre[src, pl.ds(off, tile), 0:ff].astype(f32)
        u = pre[src, pl.ds(off, tile), ff:].astype(f32)
        sigma = jax.nn.sigmoid(g)
        r = raw[at, :]
        total = jnp.sum(act[at, :].astype(f32) * r, axis=1, keepdims=True)
        score_out[src, pl.ds(off, tile), :] = jnp.broadcast_to(total, (tile, LANES))
        gr = gate_in[src, pl.ds(off, tile), 0:1].astype(f32) * r
        pgrad[src, pl.ds(off, tile), 0:ff] = (gr * u * sigma * (1.0 + g * (1.0 - sigma))).astype(
            bf16
        )
        pgrad[src, pl.ds(off, tile), ff:] = (gr * g * sigma).astype(bf16)

    pg_copy = pltpu.make_async_copy(pgrad, pg_hbm, pg_sem.at[0])
    pg_copy.start()
    for d in range(1, n_ep):
        score_copy(d, me).start()
    score_in[me] = score_out[me]

    for d in range(1, n_ed):
        hist_copy(d, lax.rem(ed + d, n_ed)).wait_recv()
    merged = jnp.max(hist_all[...], axis=0)
    ref_amax = jnp.max(merged)
    scale = 1.0 / jnp.full((1, 1), ref_amax, f32)

    for d in range(1, n_ep):
        score_copy(d, peer(d)).wait_recv()
    diagonal = lax.broadcasted_iota(jnp.int32, (cap, LANES), 0) == lax.broadcasted_iota(
        jnp.int32, (cap, LANES), 1
    )
    value0 = jnp.zeros((tokens, 1), f32)
    value1 = jnp.zeros((tokens, 1), f32)
    for e in range(n_ep):
        line = jnp.sum(jnp.where(diagonal, score_in[e], 0.0), axis=0, keepdims=True)
        found = jnp.sum(perm_t[:, e * cap : (e + 1) * cap] * line, axis=1, keepdims=True)
        value0 = value0 + jnp.where(routes_ref[:, 0:1] == e, found, 0.0)
        value1 = value1 + jnp.where(routes_ref[:, 1:2] == e, found, 0.0)
    pair = lax.broadcasted_iota(jnp.int32, (tokens, 2), 1)
    gg_out[...] = jnp.where(pair == 0, value0, value1)

    own_shard = shard[n_z - 1]
    amax_mine[...] = jnp.zeros_like(amax_mine)

    wg_copy = []
    for s in range(2):
        for way in range(2):
            there = z > 0 if way == 0 else z < n_z - 1

            @pl.when(there)
            def _():
                z_arrival(way, own_shard, s).wait_recv()

                @pl.loop(0, sub // etile)
                def _(t):
                    off = pl.multiple_of(t * etile, etile)
                    at = pl.ds(s * sub + off, etile)
                    acc[at, :] += recv[way, own_shard, s, pl.ds(off, etile), :].astype(f32)

        @pl.loop(0, sub // etile)
        def _(t):
            at = pl.ds(pl.multiple_of(s * sub + t * etile, etile), etile)
            value = acc[at, :] * scale
            acc[at, :] = value
            large = jnp.max(jnp.abs(value).reshape(etile // 8, 8, ff // LANES, LANES), axis=(0, 2))
            amax_mine[...] = jnp.maximum(amax_mine[...], large)

        copy = pltpu.make_async_copy(
            acc.at[pl.ds(s * sub, sub), :], wg_hbm.at[0, pl.ds(s * sub, sub), :], wg_sem.at[s]
        )
        copy.start()
        wg_copy.append(copy)

    for d in range(1, n_ed):
        amax_copy(d, ed).start()
    amax_all[ed] = amax_mine[...]
    for d in range(1, n_ed):
        amax_copy(d, lax.rem(ed + d, n_ed)).wait_recv()
    peak = jnp.max(amax_all[...]) * ref_amax
    width = hist_ref.shape[1]
    moved = pltpu.roll(merged, LANES - 1, 1)
    lane = lax.broadcasted_iota(jnp.int32, merged.shape, 1)
    hist_out[...] = jnp.where(lane == width - 1, peak, moved)[0:1, 0:width]

    for d in range(1, n_ep):
        for i in range(n_z):
            row_copy(i, d, me).wait_send()
        gate_copy(d, me).wait_send()
        score_copy(d, me).wait_send()
    for d in range(1, n_ed):
        hist_copy(d, ed).wait_send()
        amax_copy(d, ed).wait_send()
    w2_copy(core).wait_send()
    for i in range(n_z):
        sib_copy(i).wait_send()
    for i in range(n_z - 1):
        for s in range(2):
            z_copy(i, s).wait_send()
    pg_copy.wait()
    for copy in wg_copy:
        copy.wait()


def fused(out_grad, routes, gates, pre_acts, down_weight, history):
    f32, bf16, dma = jnp.float32, jnp.bfloat16, pltpu.SemaphoreType.DMA
    tokens, width = out_grad.shape
    ff = down_weight.shape[1]
    n_src, cap = pre_acts.shape[2], pre_acts.shape[3]
    n_ep, n_ed = lax.axis_size("ep"), lax.axis_size("ed")
    n_z = n_ed // 2
    hist = history.shape[2]
    blk = width // n_z
    half = blk // 2
    wid = blk - half // LANES * LANES
    slots = n_ep * cap
    vmem, anywhere = pl.BlockSpec(memory_space=pltpu.VMEM), pl.BlockSpec(memory_space=pl.ANY)
    pre_grad, wgrad, new_history, gate_grad = pl.pallas_call(
        functools.partial(kernel, n_z, n_ep, cap),
        out_shape=(
            jax.ShapeDtypeStruct((n_src, cap, 2 * ff), bf16),
            jax.ShapeDtypeStruct((1, half, ff), f32),
            jax.ShapeDtypeStruct((1, hist), f32),
            jax.ShapeDtypeStruct((tokens, 2), f32),
        ),
        in_specs=[vmem, vmem, vmem, anywhere, anywhere, anywhere],
        out_specs=(anywhere, anywhere, vmem, vmem),
        scratch_shapes=[
            pltpu.VMEM((n_z, tokens, blk), bf16),
            pltpu.VMEM((n_z, ff, blk), bf16),
            pltpu.VMEM((n_src, cap, 2 * ff), bf16),
            pltpu.VMEM((n_src, cap, 2 * ff), bf16),
            pltpu.VMEM((n_ep, cap, tokens), bf16),
            pltpu.VMEM((tokens, slots), f32),
            pltpu.VMEM((n_z, n_ep, cap, blk), bf16),
            pltpu.VMEM((n_z, n_ep, cap, blk), bf16),
            pltpu.VMEM((n_z, n_ep, cap, wid), bf16),
            pltpu.VMEM((2, slots, ff), bf16),
            pltpu.VMEM((slots, ff), f32),
            pltpu.VMEM((slots, ff), bf16),
            pltpu.VMEM((wid, 2 * slots), bf16),
            pltpu.VMEM((half, ff), f32),
            pltpu.VMEM((2, n_z, 2, half // 2, ff), bf16),
            pltpu.VMEM((n_z - 1, 2, half // 2, ff), bf16),
            pltpu.VMEM((n_ep, cap, LANES), bf16),
            pltpu.VMEM((n_ep, cap, LANES), bf16),
            pltpu.VMEM((n_ep, cap, LANES), f32),
            pltpu.VMEM((n_ep, cap, LANES), f32),
            pltpu.VMEM((8, LANES), f32),
            pltpu.VMEM((n_ed, 8, LANES), f32),
            pltpu.VMEM((8, LANES), f32),
            pltpu.VMEM((n_ed, 8, LANES), f32),
            dma((n_z,)),
            dma((n_z,)),
            dma((1,)),
            dma((1,)),
            dma((2,)),
            dma((n_z, n_ep)),
            dma((n_z, n_ep)),
            dma((n_ep,)),
            dma((n_ep,)),
            dma((n_ep,)),
            dma((n_ep,)),
            dma((n_z,)),
            dma((n_z,)),
            dma((1,)),
            dma((1,)),
            dma((n_z, 2)),
            dma((2, n_z, 2)),
            dma((n_ed,)),
            dma((n_ed,)),
            dma((n_ed,)),
            dma((n_ed,)),
        ],
        compiler_params=pltpu.CompilerParams(
            collective_id=0, has_side_effects=True, vmem_limit_bytes=56 * 1024 * 1024
        ),
        cost_estimate=pl.CostEstimate(
            flops=4 * slots * width * ff, bytes_accessed=16 * 1024 * 1024, transcendentals=slots * ff
        ),
    )(
        routes, gates, history[0], out_grad, pre_acts[0, 0], down_weight
    )
    return pre_grad[None, None], wgrad, new_history, gate_grad


def body(out_grad, routes, gates, pre_acts, down_weight, history):
    tokens, width = out_grad.shape
    cap = pre_acts.shape[3]
    n_ed = lax.axis_size("ed")
    fits = (
        n_ed % 2 == 0
        and n_ed > 2
        and cap == LANES
        and tokens == LANES
        and down_weight.shape[0] == 1
        and width % (n_ed // 2 * LANES) == 0
        and width // n_ed % 64 == 0
    )
    run = fused if fits else plain
    return run(out_grad, routes, gates, pre_acts, down_weight, history)


def solution(mesh):
    placed = (
        P(("ed", "ep"), None),
        P(("ed", "ep"), None),
        P(("ed", "ep"), None),
        P("ed", "ep", None, None, None),
        P("ep", None, None),
        P("ed", "ep", None),
    )
    return jax.shard_map(
        body,
        mesh=mesh,
        in_specs=placed,
        out_specs=(
            P("ed", "ep", None, None, None),
            P("ep", "ed", None),
            P("ep", None),
            P(("ed", "ep"), None),
        ),
        check_vma=False,
    )
```

```python
import functools

import jax
import jax.numpy as jnp
from jax import lax
from jax.experimental import pallas as pl
from jax.experimental.pallas import tpu as pltpu
from jax.sharding import PartitionSpec as P


def split_pre(pre_block, width_ff):
    gate_pre = pre_block[:, :width_ff].astype(jnp.float32)
    up_pre = pre_block[:, width_ff:].astype(jnp.float32)
    return (gate_pre, up_pre, jax.nn.sigmoid(gate_pre))


def plain(out_grad, routes, gates, pre_acts, down_weight, history):
    tok_rows, top = routes.shape
    width = out_grad.shape[1]
    local = down_weight.shape[0]
    width_ff = down_weight.shape[1]
    n_src = pre_acts.shape[2]
    cap = pre_acts.shape[3]
    n_ep = lax.axis_size("ep")
    n_replicas = lax.axis_size("ed")
    experts = local * n_ep
    flat = routes.reshape(-1)
    hits = (flat[:, None] == jnp.arange(experts, dtype=jnp.int32)[None, :]).astype(jnp.int32)
    before = jnp.cumsum(hits, axis=0) - hits
    slot = jnp.sum(before * hits, axis=1)
    target = flat * cap + slot
    owner = jnp.arange(tok_rows * top, dtype=jnp.int32) // top
    table = jnp.zeros((experts * cap,), jnp.int32).at[target].set(owner + 1)
    picked = out_grad[jnp.maximum(table - 1, 0)]
    send_rows = jnp.where((table > 0)[:, None], picked, jnp.zeros_like(picked))
    send_gate = jnp.zeros((experts * cap,), jnp.bfloat16).at[target].set(gates.reshape(-1))
    arrived, arrived_gate = (
        lax.all_to_all(
            send_rows.reshape(n_ep, local * cap, width),
            "ep",
            split_axis=0,
            concat_axis=0,
            tiled=True,
        ),
        lax.all_to_all(
            send_gate.reshape(n_ep, local * cap), "ep", split_axis=0, concat_axis=0, tiled=True
        ),
    )
    arrived = (
        arrived.reshape(n_ep, local, cap, width)
        .transpose(1, 0, 2, 3)
        .reshape(local, n_ep * cap, width)
    )
    arrived_gate = (
        arrived_gate.reshape(n_ep, local, cap)
        .transpose(1, 0, 2)
        .reshape(local, n_ep * cap)
        .astype(jnp.float32)
    )
    merged = lax.pmax(history, "ed")[0]
    ref_amax = jnp.max(merged, axis=1)
    scale = 1.0 / ref_amax
    rows = arrived[0]
    gate_row = arrived_gate[0][:, None]
    weight = down_weight[0]
    pre_block = pre_acts[0, 0].reshape(n_src * cap, 2 * width_ff)
    gate_pre, up_pre, sigma = split_pre(pre_block, width_ff)
    act = (gate_pre * sigma * up_pre).astype(jnp.bfloat16)
    weighted = (gate_row * act.astype(jnp.float32)).astype(jnp.bfloat16)
    raw = jnp.einsum("rd,hd->rh", rows, weight, preferred_element_type=jnp.float32)
    score = jnp.sum(act.astype(jnp.float32) * raw, axis=1)
    grad_act = gate_row * raw
    grad_gate = grad_act * up_pre * sigma * (1.0 + gate_pre * (1.0 - sigma))
    grad_up = grad_act * gate_pre * sigma
    grads_pre = [
        jnp.concatenate([grad_gate, grad_up], axis=1)
        .astype(jnp.bfloat16)
        .reshape(n_src, cap, 2 * width_ff)
    ]
    scores = [score.reshape(n_ep, cap)]
    factor = scale[0]

    def term(start, count, rows=rows, weighted=weighted, factor=factor):
        return factor * jnp.einsum("rd,rh->dh", rows, weighted, preferred_element_type=jnp.float32)

    shard = lax.psum_scatter(
        term(jnp.int32(0), width // n_replicas * lax.axis_size("ed")).astype(jnp.bfloat16),
        "ed",
        scatter_dimension=0,
        tiled=True,
    ).astype(jnp.float32)
    shards = [shard]
    wgrad = jnp.stack(shards)
    peak = lax.pmax(jnp.max(jnp.abs(wgrad), axis=(1, 2)), "ed")
    new_amax = peak * ref_amax
    new_history = jnp.concatenate([merged[:, 1:], new_amax[:, None]], axis=1)
    pre_grad = jnp.stack(grads_pre)[None]
    outgoing = jnp.stack(scores).transpose(1, 0, 2).reshape(n_ep, local * cap)
    returned = lax.all_to_all(outgoing, "ep", split_axis=0, concat_axis=0, tiled=True)
    gate_grad = returned.reshape(-1)[target].reshape(tok_rows, top)
    return (pre_grad, wgrad, new_history, gate_grad)


MESH = pl.DeviceIdType.MESH
LANES = 128


def orders(n_z):
    centre = (n_z - 1) / 2
    return [
        sorted(range(n_z), key=lambda j: (-abs(j - z), -abs(j - centre), j)) for z in range(n_z)
    ]


def split_half(half):
    big = -(-half // (2 * LANES)) * LANES
    small = half - big
    return big, small, -(-small // LANES) * LANES


def kernel(
    n_z,
    n_ep,
    cap,
    routes_ref,
    gates_ref,
    hist_ref,
    tok_hbm,
    pre_hbm,
    w_hbm,
    pgrad,
    wg_out,
    hist_out,
    gg_out,
    tok,
    wv,
    pre,
    perm,
    perm_t,
    outrows,
    rows,
    sib,
    w2,
    raw,
    act,
    rt,
    acc,
    recv,
    zsend,
    gate_out,
    gate_in,
    score_out,
    score_in,
    hist_mine,
    hist_all,
    amax_mine,
    amax_all,
    tok_sem,
    w_sem,
    pre_sem,
    row_ss,
    row_rs,
    gate_ss,
    gate_rs,
    score_ss,
    score_rs,
    sib_ss,
    sib_rs,
    w2_ss,
    w2_rs,
    z_ss,
    z_rs,
    hist_ss,
    hist_rs,
    amax_ss,
    amax_rs,
):
    f32, bf16 = jnp.float32, jnp.bfloat16
    ed, me = lax.axis_index("ed"), lax.axis_index("ep")
    z, core = ed // 2, ed % 2
    n_ed = 2 * n_z
    sibling = z * 2 + 1 - core
    blk = tok.shape[2]
    half = blk // 2
    big, small, win = split_half(half)
    rest = blk - 2 * big
    slots = n_ep * cap
    ff = act.shape[1]
    table = orders(n_z)

    def shard_at(i):
        j = jnp.int32(table[0][i])
        for at in range(1, n_z):
            j = jnp.where(z == at, jnp.int32(table[at][i]), j)
        return j

    shard = [shard_at(i) for i in range(n_z)]

    pieces = ((0, 0, big), (blk - big, big, big), (big, 2 * big, rest))

    def columns(i, begin, count):
        return pl.ds(pl.multiple_of(shard[i] * blk + begin, LANES), count)

    tok_in = [
        [
            pltpu.make_async_copy(
                tok_hbm.at[:, columns(i, begin, count)],
                tok.at[i, :, pl.ds(to, count)],
                tok_sem.at[i, p],
            )
            for p, (begin, to, count) in enumerate(pieces)
        ]
        for i in range(n_z)
    ]
    w_in = [
        [
            pltpu.make_async_copy(
                w_hbm.at[0, :, columns(i, begin, count)],
                wv.at[i, :, pl.ds(to, count)],
                w_sem.at[i, p],
            )
            for p, (begin, to, count) in enumerate(pieces)
        ]
        for i in range(n_z)
    ]
    pre_in = pltpu.make_async_copy(pre_hbm, pre, pre_sem.at[0])
    for copy in tok_in[0]:
        copy.start()
    pre_in.start()
    for i in range(1, n_z):
        for copy in tok_in[i]:
            copy.start()
    for i in range(n_z):
        for copy in w_in[i]:
            copy.start()

    barrier = pltpu.get_barrier_semaphore()
    for d in range(1, n_ep):
        pl.semaphore_signal(
            barrier, inc=1, device_id={"ep": lax.rem(me + d, n_ep)}, device_id_type=MESH
        )
    for d in range(1, n_ed):
        pl.semaphore_signal(
            barrier, inc=1, device_id={"ed": lax.rem(ed + d, n_ed)}, device_id_type=MESH
        )

    hist_mine[...] = jnp.zeros_like(hist_mine)
    hist_mine[0:1, 0 : hist_ref.shape[1]] = hist_ref[...]

    tokens = tok.shape[1]
    first, second = routes_ref[0:1, :], routes_ref[1:2, :]
    gate0, gate1 = gates_ref[0:1, :].astype(f32), gates_ref[1:2, :].astype(f32)
    expert = lax.broadcasted_iota(jnp.int32, (16, tokens), 0)
    hits = jnp.where(first == expert, 1.0, 0.0) + jnp.where(second == expert, 1.0, 0.0)
    earlier = lax.broadcasted_iota(jnp.int32, (tokens, tokens), 0) < lax.broadcasted_iota(
        jnp.int32, (tokens, tokens), 1
    )
    slot = jnp.dot(
        hits.astype(bf16), jnp.where(earlier, 1.0, 0.0).astype(bf16), preferred_element_type=f32
    )
    place = lax.broadcasted_iota(jnp.int32, (cap, tokens), 0).astype(f32)
    for e in range(n_ep):
        own = jnp.where(slot[e : e + 1, :] == place, hits[e : e + 1, :], 0.0)
        perm_t[e] = own
        perm[e] = own.astype(bf16)
        gate = jnp.where(first == e, gate0, 0.0) + jnp.where(second == e, gate1, 0.0)
        column = jnp.sum(own * gate, axis=1, keepdims=True)
        gate_out[e] = jnp.broadcast_to(column, (cap, LANES)).astype(bf16)
    gate_in[me] = gate_out[me]

    def place_rows(i):
        for copy in tok_in[i]:
            copy.wait()

        @pl.loop(0, n_ep)
        def _(e):
            outrows[i, e] = jnp.dot(perm[e], tok[i], preferred_element_type=f32).astype(bf16)

        rows[i, me] = outrows[i, me]

    place_rows(0)
    pl.semaphore_wait(barrier, n_ep - 1 + n_ed - 1)

    def to_ep(src, dst, ss, rs, d):
        return pltpu.make_async_remote_copy(
            src_ref=src, dst_ref=dst, send_sem=ss, recv_sem=rs,
            device_id={"ep": lax.rem(me + d, n_ep)}, device_id_type=MESH,
        )

    def to_ed(src, dst, ss, rs, target):
        return pltpu.make_async_remote_copy(
            src_ref=src, dst_ref=dst, send_sem=ss, recv_sem=rs,
            device_id={"ed": target}, device_id_type=MESH,
        )

    def peer(d):
        return lax.rem(me + d, n_ep)

    spans = (pl.ds(0, 2 * big), pl.ds(2 * big, rest))

    def row_copy(i, a, d, src):
        return to_ep(
            outrows.at[i, peer(d), :, spans[a]], rows.at[i, src, :, spans[a]],
            row_ss.at[i, a, d], row_rs.at[i, a, src], d,
        )

    def gate_copy(d, src):
        return to_ep(gate_out.at[peer(d)], gate_in.at[src], gate_ss.at[d], gate_rs.at[src], d)

    def score_copy(d, src):
        return to_ep(score_out.at[peer(d)], score_in.at[src], score_ss.at[d], score_rs.at[src], d)

    def hist_copy(d, src):
        return to_ed(
            hist_mine, hist_all.at[src], hist_ss.at[d], hist_rs.at[src], lax.rem(ed + d, n_ed)
        )

    def amax_copy(d, src):
        return to_ed(
            amax_mine, amax_all.at[src], amax_ss.at[d], amax_rs.at[src], lax.rem(ed + d, n_ed)
        )

    def dispatch(i, a):
        for d in range(1, n_ep):
            row_copy(i, a, d, me).start()

    dispatch(0, 0)
    for d in range(1, n_ep):
        gate_copy(d, me).start()
    for d in range(1, n_ed):
        hist_copy(d, ed).start()
    hist_all[ed] = hist_mine[...]

    @pl.when(z == 0)
    def _():
        recv[0, z] = jnp.zeros(recv.shape[2:], bf16)

    @pl.when(z == n_z - 1)
    def _():
        recv[1, z] = jnp.zeros(recv.shape[2:], bf16)

    place_rows(1)

    tile = 32
    pre_in.wait()
    for d in range(1, n_ep):
        gate_copy(d, peer(d)).wait_recv()

    @pl.loop(0, slots // tile)
    def _(t):
        at = pl.ds(pl.multiple_of(t * tile, tile), tile)
        src, off = t // (cap // tile), t % (cap // tile)
        off = pl.multiple_of(off * tile, tile)
        g = pre[src, pl.ds(off, tile), 0:ff].astype(f32)
        u = pre[src, pl.ds(off, tile), ff:].astype(f32)
        a = (g * jax.nn.sigmoid(g) * u).astype(bf16)
        act[at, :] = a
        gate = gate_in[src, pl.ds(off, tile), 0:1].astype(f32)
        w2[core, at, :] = (gate * a.astype(f32)).astype(bf16)

    def w2_copy(which):
        return to_ed(w2.at[which], w2.at[which], w2_ss.at[0], w2_rs.at[0], sibling)

    w2_copy(core).start()

    def window(a, which):
        if a == 0:
            return pl.ds(pl.multiple_of(which * big, LANES), big)
        return pl.ds(pl.multiple_of(2 * big + which * (rest - win), LANES), win)

    heights = (big, small)
    starts = (0, big)
    wide = (big, win)

    def sib_copy(i, a):
        return to_ed(
            rows.at[i, :, :, window(a, 1 - core)], sib.at[i, a, :, :, pl.ds(0, wide[a])],
            sib_ss.at[i, a], sib_rs.at[i, a], sibling,
        )

    def z_copy(i, s):
        right = shard[i] > z
        target = jnp.where(right, z + 1, z - 1)
        way = jnp.where(right, 0, 1)
        at = pl.ds(starts[s], heights[s])
        return to_ed(
            zsend.at[i, at], recv.at[way, shard[i], at], z_ss.at[i, s],
            z_rs.at[way, shard[i], s], target * 2 + core,
        )

    def z_arrival(way, j, s):
        at = pl.ds(starts[s], heights[s])
        return to_ed(
            zsend.at[0, at], recv.at[way, j, at], z_ss.at[0, 0], z_rs.at[way, j, s], sibling
        )

    n_tile = 256
    etile = 32

    def part(i, a):
        sib_copy(i, a).start()
        rt[0 : wide[a], pl.ds(pl.multiple_of(core * slots, LANES), slots)] = (
            rows[i, :, :, window(a, core)].reshape(slots, wide[a]).T
        )
        if i == 0 and a == 0:
            w2_copy(1 - core).wait_recv()
        sib_copy(i, a).wait_recv()
        rt[0 : wide[a], pl.ds(pl.multiple_of((1 - core) * slots, LANES), slots)] = (
            sib[i, a, :, :, 0 : wide[a]].reshape(slots, wide[a]).T
        )
        skip = 0 if a == 0 else pl.multiple_of((small - (rest - win)) * core, 16)

        @pl.loop(0, ff // n_tile)
        def _(n):
            at = pl.ds(pl.multiple_of(n * n_tile, n_tile), n_tile)
            acc[starts[a] : starts[a] + heights[a], at] = jnp.dot(
                rt[pl.ds(skip, heights[a]), :],
                w2[:, :, at].reshape(2 * slots, n_tile),
                preferred_element_type=f32,
            )

    def send_on(i, s, came_by):
        @pl.loop(0, heights[s] // etile)
        def _(t):
            at = pl.ds(pl.multiple_of(starts[s] + t * etile, etile), etile)
            value = acc[at, :]
            if came_by is not None:
                value = value + recv[came_by, shard[i], at, :].astype(f32)
            zsend[i, at, :] = value.astype(bf16)

        if i > 0:
            z_copy(i - 1, s).wait_send()
        z_copy(i, s).start()

    for i in range(n_z):
        last = i == n_z - 1
        right = shard[i] > z
        way = jnp.where(right, 0, 1)
        fed = jnp.where(right, z > 0, z < n_z - 1)
        for a in range(2):
            for d in range(1, n_ep):
                row_copy(i, a, d, peer(d)).wait_recv()
            if i == 0 and a == 0:
                dispatch(0, 1)
            if not last and a == 1:
                dispatch(i + 1, 0)
                dispatch(i + 1, 1)
            part(i, a)
            if not last:

                @pl.when(jnp.logical_not(fed))
                def _():
                    send_on(i, a, None)

        for copy in w_in[i]:
            copy.wait()

        @pl.loop(0, ff // n_tile)
        def _(n):
            at = pl.ds(pl.multiple_of(n * n_tile, n_tile), n_tile)
            got = lax.dot_general(
                rows[i].reshape(slots, blk), wv[i, at, :], (((1,), (1,)), ((), ())),
                preferred_element_type=f32,
            )
            if i == 0:
                raw[:, at] = got
            else:
                raw[:, at] += got

        if i + 2 < n_z:
            place_rows(i + 2)
        if last:
            break

        @pl.when(fed)
        def _():
            for s in range(2):
                z_arrival(way, shard[i], s).wait_recv()
                send_on(i, s, way)

    @pl.loop(0, slots // tile)
    def _(t):
        at = pl.ds(pl.multiple_of(t * tile, tile), tile)
        src, off = t // (cap // tile), t % (cap // tile)
        off = pl.multiple_of(off * tile, tile)
        g = pre[src, pl.ds(off, tile), 0:ff].astype(f32)
        u = pre[src, pl.ds(off, tile), ff:].astype(f32)
        sigma = jax.nn.sigmoid(g)
        r = raw[at, :]
        total = jnp.sum(act[at, :].astype(f32) * r, axis=1, keepdims=True)
        score_out[src, pl.ds(off, tile), :] = jnp.broadcast_to(total, (tile, LANES))
        gr = gate_in[src, pl.ds(off, tile), 0:1].astype(f32) * r
        pgrad[src, pl.ds(off, tile), 0:ff] = (gr * u * sigma * (1.0 + g * (1.0 - sigma))).astype(
            bf16
        )
        pgrad[src, pl.ds(off, tile), ff:] = (gr * g * sigma).astype(bf16)

    for d in range(1, n_ep):
        score_copy(d, me).start()
    score_in[me] = score_out[me]

    for d in range(1, n_ed):
        hist_copy(d, lax.rem(ed + d, n_ed)).wait_recv()
    merged = jnp.max(hist_all[...], axis=0)
    ref_amax = jnp.max(merged)
    scale = 1.0 / jnp.full((1, 1), ref_amax, f32)

    for d in range(1, n_ep):
        score_copy(d, peer(d)).wait_recv()
    value0 = jnp.zeros((1, tokens), f32)
    value1 = jnp.zeros((1, tokens), f32)
    for e in range(n_ep):
        found = jnp.sum(perm_t[e] * score_in[e], axis=0, keepdims=True)
        value0 = value0 + jnp.where(first == e, found, 0.0)
        value1 = value1 + jnp.where(second == e, found, 0.0)
    gg_out[0:1, :] = value0
    gg_out[1:2, :] = value1

    amax_mine[...] = jnp.zeros_like(amax_mine)
    for s in range(2):

        @pl.when(z > 0)
        def _():
            z_arrival(0, z, s).wait_recv()

        @pl.when(z < n_z - 1)
        def _():
            z_arrival(1, z, s).wait_recv()

        base = core * small if s == 0 else (1 - core) * big

        @pl.loop(0, heights[s] // etile)
        def _(t):
            at = pl.ds(pl.multiple_of(starts[s] + t * etile, etile), etile)
            came = recv[0, z, at, :].astype(f32) + recv[1, z, at, :].astype(f32)
            value = (acc[at, :] + came) * scale
            wg_out[0, pl.ds(pl.multiple_of(base + t * etile, etile), etile), :] = value
            large = jnp.max(jnp.abs(value).reshape(etile // 8, 8, ff // LANES, LANES), axis=(0, 2))
            amax_mine[...] = jnp.maximum(amax_mine[...], large)

    for d in range(1, n_ed):
        amax_copy(d, ed).start()
    amax_all[ed] = amax_mine[...]
    for d in range(1, n_ed):
        amax_copy(d, lax.rem(ed + d, n_ed)).wait_recv()
    peak = jnp.max(amax_all[...]) * ref_amax
    width = hist_ref.shape[1]
    moved = pltpu.roll(merged, LANES - 1, 1)
    lane = lax.broadcasted_iota(jnp.int32, merged.shape, 1)
    hist_out[...] = jnp.where(lane == width - 1, peak, moved)[0:1, 0:width]

    for d in range(1, n_ep):
        for i in range(n_z):
            for a in range(2):
                row_copy(i, a, d, me).wait_send()
        gate_copy(d, me).wait_send()
        score_copy(d, me).wait_send()
    for d in range(1, n_ed):
        hist_copy(d, ed).wait_send()
        amax_copy(d, ed).wait_send()
    w2_copy(core).wait_send()
    for i in range(n_z):
        for a in range(2):
            sib_copy(i, a).wait_send()
    for s in range(2):
        z_copy(n_z - 2, s).wait_send()


def fused(out_grad, routes, gates, pre_acts, down_weight, history):
    f32, bf16, dma = jnp.float32, jnp.bfloat16, pltpu.SemaphoreType.DMA
    tokens, width = out_grad.shape
    ff = down_weight.shape[1]
    n_src, cap = pre_acts.shape[2], pre_acts.shape[3]
    n_ep, n_ed = lax.axis_size("ep"), lax.axis_size("ed")
    n_z = n_ed // 2
    hist = history.shape[2]
    blk = width // n_z
    half = blk // 2
    big, small, win = split_half(half)
    slots = n_ep * cap
    vmem, anywhere = pl.BlockSpec(memory_space=pltpu.VMEM), pl.BlockSpec(memory_space=pl.ANY)
    pre_grad, wgrad, new_history, gate_grad = pl.pallas_call(
        functools.partial(kernel, n_z, n_ep, cap),
        out_shape=(
            pltpu.VMEM((n_src, cap, 2 * ff), bf16),
            pltpu.VMEM((1, half, ff), f32),
            jax.ShapeDtypeStruct((1, hist), f32),
            jax.ShapeDtypeStruct((2, tokens), f32),
        ),
        in_specs=[vmem, vmem, vmem, anywhere, anywhere, anywhere],
        out_specs=(vmem, vmem, vmem, vmem),
        scratch_shapes=[
            pltpu.VMEM((n_z, tokens, blk), bf16),
            pltpu.VMEM((n_z, ff, blk), bf16),
            pltpu.VMEM((n_src, cap, 2 * ff), bf16),
            pltpu.VMEM((n_ep, cap, tokens), bf16),
            pltpu.VMEM((n_ep, cap, tokens), f32),
            pltpu.VMEM((n_z, n_ep, cap, blk), bf16),
            pltpu.VMEM((n_z, n_ep, cap, blk), bf16),
            pltpu.VMEM((n_z, 2, n_ep, cap, max(big, win)), bf16),
            pltpu.VMEM((2, slots, ff), bf16),
            pltpu.VMEM((slots, ff), f32),
            pltpu.VMEM((slots, ff), bf16),
            pltpu.VMEM((max(big, win), 2 * slots), bf16),
            pltpu.VMEM((half, ff), f32),
            pltpu.VMEM((2, n_z, half, ff), bf16),
            pltpu.VMEM((n_z - 1, half, ff), bf16),
            pltpu.VMEM((n_ep, cap, LANES), bf16),
            pltpu.VMEM((n_ep, cap, LANES), bf16),
            pltpu.VMEM((n_ep, cap, LANES), f32),
            pltpu.VMEM((n_ep, cap, LANES), f32),
            pltpu.VMEM((8, LANES), f32),
            pltpu.VMEM((n_ed, 8, LANES), f32),
            pltpu.VMEM((8, LANES), f32),
            pltpu.VMEM((n_ed, 8, LANES), f32),
            dma((n_z, 3)),
            dma((n_z, 3)),
            dma((1,)),
            dma((n_z, 2, n_ep)),
            dma((n_z, 2, n_ep)),
            dma((n_ep,)),
            dma((n_ep,)),
            dma((n_ep,)),
            dma((n_ep,)),
            dma((n_z, 2)),
            dma((n_z, 2)),
            dma((1,)),
            dma((1,)),
            dma((n_z, 2)),
            dma((2, n_z, 2)),
            dma((n_ed,)),
            dma((n_ed,)),
            dma((n_ed,)),
            dma((n_ed,)),
        ],
        compiler_params=pltpu.CompilerParams(
            collective_id=0, has_side_effects=True, vmem_limit_bytes=56 * 1024 * 1024
        ),
        cost_estimate=pl.CostEstimate(
            flops=4 * slots * width * ff, bytes_accessed=16 * 1024 * 1024, transcendentals=slots * ff
        ),
    )(
        routes.T, gates.T, history[0], out_grad, pre_acts[0, 0], down_weight
    )
    return pre_grad[None, None], wgrad, new_history, gate_grad.T


def body(out_grad, routes, gates, pre_acts, down_weight, history):
    tokens, width = out_grad.shape
    cap = pre_acts.shape[3]
    n_ed = lax.axis_size("ed")
    fits = (
        n_ed % 2 == 0
        and n_ed > 2
        and cap == LANES
        and tokens == LANES
        and down_weight.shape[0] == 1
        and width % (n_ed // 2 * LANES) == 0
        and width // n_ed % 64 == 0
        and lax.axis_size("ep") <= 16
    )
    run = fused if fits else plain
    return run(out_grad, routes, gates, pre_acts, down_weight, history)


def solution(mesh):
    placed = (
        P(("ed", "ep"), None),
        P(("ed", "ep"), None),
        P(("ed", "ep"), None),
        P("ed", "ep", None, None, None),
        P("ep", None, None),
        P("ed", "ep", None),
    )
    return jax.shard_map(
        body,
        mesh=mesh,
        in_specs=placed,
        out_specs=(
            P("ed", "ep", None, None, None),
            P("ep", "ed", None),
            P("ep", None),
            P(("ed", "ep"), None),
        ),
        check_vma=False,
    )
```

```python
import functools

import jax
import jax.numpy as jnp
from jax import lax
from jax.experimental import pallas as pl
from jax.experimental.pallas import tpu as pltpu
from jax.sharding import PartitionSpec as P


def split_pre(pre_block, width_ff):
    gate_pre = pre_block[:, :width_ff].astype(jnp.float32)
    up_pre = pre_block[:, width_ff:].astype(jnp.float32)
    return (gate_pre, up_pre, jax.nn.sigmoid(gate_pre))


def plain(out_grad, routes, gates, pre_acts, down_weight, history):
    tok_rows, top = routes.shape
    width = out_grad.shape[1]
    local = down_weight.shape[0]
    width_ff = down_weight.shape[1]
    n_src = pre_acts.shape[2]
    cap = pre_acts.shape[3]
    n_ep = lax.axis_size("ep")
    n_replicas = lax.axis_size("ed")
    experts = local * n_ep
    flat = routes.reshape(-1)
    hits = (flat[:, None] == jnp.arange(experts, dtype=jnp.int32)[None, :]).astype(jnp.int32)
    before = jnp.cumsum(hits, axis=0) - hits
    slot = jnp.sum(before * hits, axis=1)
    target = flat * cap + slot
    owner = jnp.arange(tok_rows * top, dtype=jnp.int32) // top
    table = jnp.zeros((experts * cap,), jnp.int32).at[target].set(owner + 1)
    picked = out_grad[jnp.maximum(table - 1, 0)]
    send_rows = jnp.where((table > 0)[:, None], picked, jnp.zeros_like(picked))
    send_gate = jnp.zeros((experts * cap,), jnp.bfloat16).at[target].set(gates.reshape(-1))
    arrived, arrived_gate = (
        lax.all_to_all(
            send_rows.reshape(n_ep, local * cap, width),
            "ep",
            split_axis=0,
            concat_axis=0,
            tiled=True,
        ),
        lax.all_to_all(
            send_gate.reshape(n_ep, local * cap), "ep", split_axis=0, concat_axis=0, tiled=True
        ),
    )
    arrived = (
        arrived.reshape(n_ep, local, cap, width)
        .transpose(1, 0, 2, 3)
        .reshape(local, n_ep * cap, width)
    )
    arrived_gate = (
        arrived_gate.reshape(n_ep, local, cap)
        .transpose(1, 0, 2)
        .reshape(local, n_ep * cap)
        .astype(jnp.float32)
    )
    merged = lax.pmax(history, "ed")[0]
    ref_amax = jnp.max(merged, axis=1)
    scale = 1.0 / ref_amax
    rows = arrived[0]
    gate_row = arrived_gate[0][:, None]
    weight = down_weight[0]
    pre_block = pre_acts[0, 0].reshape(n_src * cap, 2 * width_ff)
    gate_pre, up_pre, sigma = split_pre(pre_block, width_ff)
    act = (gate_pre * sigma * up_pre).astype(jnp.bfloat16)
    weighted = (gate_row * act.astype(jnp.float32)).astype(jnp.bfloat16)
    raw = jnp.einsum("rd,hd->rh", rows, weight, preferred_element_type=jnp.float32)
    score = jnp.sum(act.astype(jnp.float32) * raw, axis=1)
    grad_act = gate_row * raw
    grad_gate = grad_act * up_pre * sigma * (1.0 + gate_pre * (1.0 - sigma))
    grad_up = grad_act * gate_pre * sigma
    grads_pre = [
        jnp.concatenate([grad_gate, grad_up], axis=1)
        .astype(jnp.bfloat16)
        .reshape(n_src, cap, 2 * width_ff)
    ]
    scores = [score.reshape(n_ep, cap)]
    factor = scale[0]

    def term(start, count, rows=rows, weighted=weighted, factor=factor):
        return factor * jnp.einsum("rd,rh->dh", rows, weighted, preferred_element_type=jnp.float32)

    shard = lax.psum_scatter(
        term(jnp.int32(0), width // n_replicas * lax.axis_size("ed")).astype(jnp.bfloat16),
        "ed",
        scatter_dimension=0,
        tiled=True,
    ).astype(jnp.float32)
    shards = [shard]
    wgrad = jnp.stack(shards)
    peak = lax.pmax(jnp.max(jnp.abs(wgrad), axis=(1, 2)), "ed")
    new_amax = peak * ref_amax
    new_history = jnp.concatenate([merged[:, 1:], new_amax[:, None]], axis=1)
    pre_grad = jnp.stack(grads_pre)[None]
    outgoing = jnp.stack(scores).transpose(1, 0, 2).reshape(n_ep, local * cap)
    returned = lax.all_to_all(outgoing, "ep", split_axis=0, concat_axis=0, tiled=True)
    gate_grad = returned.reshape(-1)[target].reshape(tok_rows, top)
    return (pre_grad, wgrad, new_history, gate_grad)


MESH = pl.DeviceIdType.MESH
LANES = 128


def orders(n_z):
    centre = (n_z - 1) / 2
    return [
        sorted(range(n_z), key=lambda j: (-abs(j - z), -abs(j - centre), j)) for z in range(n_z)
    ]


def split_half(half):
    whole = max(half // LANES - 1, 0)
    small = half - whole * LANES
    return whole, small, -(-small // LANES) * LANES


def kernel(
    n_z,
    n_ep,
    cap,
    routes_ref,
    gates_ref,
    hist_ref,
    tok_hbm,
    pre_hbm,
    w_hbm,
    pgrad,
    wg_out,
    hist_out,
    gg_out,
    tok,
    wv,
    pre,
    perm,
    perm_t,
    outrows,
    rows,
    sib,
    w2,
    raw,
    act,
    rt,
    acc,
    recv,
    zsend,
    gate_out,
    gate_in,
    score_out,
    score_in,
    hist_mine,
    hist_all,
    amax_mine,
    amax_all,
    tok_sem,
    w_sem,
    pre_sem,
    row_ss,
    row_rs,
    gate_ss,
    gate_rs,
    score_ss,
    score_rs,
    sib_ss,
    sib_rs,
    w2_ss,
    w2_rs,
    z_ss,
    z_rs,
    hist_ss,
    hist_rs,
    amax_ss,
    amax_rs,
):
    f32, bf16 = jnp.float32, jnp.bfloat16
    ed, me = lax.axis_index("ed"), lax.axis_index("ep")
    z, core = ed // 2, ed % 2
    n_ed = 2 * n_z
    sibling = z * 2 + 1 - core
    blk = tok.shape[2]
    half = blk // 2
    whole, small, win = split_half(half)
    parts = whole + 1
    lead = 2 * whole * LANES
    rest = blk - lead
    slots = n_ep * cap
    ff = act.shape[1]
    table = orders(n_z)

    def shard_at(i):
        j = jnp.int32(table[0][i])
        for at in range(1, n_z):
            j = jnp.where(z == at, jnp.int32(table[at][i]), j)
        return j

    shard = [shard_at(i) for i in range(n_z)]

    pieces = []
    for a in range(whole):
        pieces.append((a * LANES, 2 * a * LANES, LANES))
        pieces.append((blk - (a + 1) * LANES, (2 * a + 1) * LANES, LANES))
    pieces.append((whole * LANES, lead, rest))

    def columns(i, begin, count):
        return pl.ds(pl.multiple_of(shard[i] * blk + begin, LANES), count)

    tok_in = [
        [
            pltpu.make_async_copy(
                tok_hbm.at[:, columns(i, begin, count)],
                tok.at[i, :, pl.ds(to, count)],
                tok_sem.at[i, p],
            )
            for p, (begin, to, count) in enumerate(pieces)
        ]
        for i in range(n_z)
    ]
    w_in = [
        [
            pltpu.make_async_copy(
                w_hbm.at[0, :, columns(i, begin, count)],
                wv.at[i, :, pl.ds(to, count)],
                w_sem.at[i, p],
            )
            for p, (begin, to, count) in enumerate(pieces)
        ]
        for i in range(n_z)
    ]
    pre_in = pltpu.make_async_copy(pre_hbm, pre, pre_sem.at[0])
    for copy in tok_in[0]:
        copy.start()
    pre_in.start()
    for i in range(1, n_z):
        for copy in tok_in[i]:
            copy.start()
    for i in range(n_z):
        for copy in w_in[i]:
            copy.start()

    barrier = pltpu.get_barrier_semaphore()
    for d in range(1, n_ep):
        pl.semaphore_signal(
            barrier, inc=1, device_id={"ep": lax.rem(me + d, n_ep)}, device_id_type=MESH
        )
    for d in range(1, n_ed):
        pl.semaphore_signal(
            barrier, inc=1, device_id={"ed": lax.rem(ed + d, n_ed)}, device_id_type=MESH
        )

    hist_mine[...] = jnp.zeros_like(hist_mine)
    hist_mine[0:1, 0 : hist_ref.shape[1]] = hist_ref[...]

    tokens = tok.shape[1]
    first, second = routes_ref[0:1, :], routes_ref[1:2, :]
    gate0, gate1 = gates_ref[0:1, :].astype(f32), gates_ref[1:2, :].astype(f32)
    expert = lax.broadcasted_iota(jnp.int32, (16, tokens), 0)
    hits = jnp.where(first == expert, 1.0, 0.0) + jnp.where(second == expert, 1.0, 0.0)
    earlier = lax.broadcasted_iota(jnp.int32, (tokens, tokens), 0) < lax.broadcasted_iota(
        jnp.int32, (tokens, tokens), 1
    )
    slot = jnp.dot(
        hits.astype(bf16), jnp.where(earlier, 1.0, 0.0).astype(bf16), preferred_element_type=f32
    )
    place = lax.broadcasted_iota(jnp.int32, (cap, tokens), 0).astype(f32)
    for e in range(n_ep):
        own = jnp.where(slot[e : e + 1, :] == place, hits[e : e + 1, :], 0.0)
        perm_t[e] = own
        perm[e] = own.astype(bf16)
        gate = jnp.where(first == e, gate0, 0.0) + jnp.where(second == e, gate1, 0.0)
        column = jnp.sum(own * gate, axis=1, keepdims=True)
        gate_out[e] = jnp.broadcast_to(column, (cap, LANES)).astype(bf16)
    gate_in[me] = gate_out[me]

    def place_rows(i):
        for copy in tok_in[i]:
            copy.wait()

        @pl.loop(0, n_ep)
        def _(e):
            outrows[i, e] = jnp.dot(perm[e], tok[i], preferred_element_type=f32).astype(bf16)

        rows[i, me] = outrows[i, me]

    place_rows(0)
    pl.semaphore_wait(barrier, n_ep - 1 + n_ed - 1)

    def to_ep(src, dst, ss, rs, d):
        return pltpu.make_async_remote_copy(
            src_ref=src, dst_ref=dst, send_sem=ss, recv_sem=rs,
            device_id={"ep": lax.rem(me + d, n_ep)}, device_id_type=MESH,
        )

    def to_ed(src, dst, ss, rs, target):
        return pltpu.make_async_remote_copy(
            src_ref=src, dst_ref=dst, send_sem=ss, recv_sem=rs,
            device_id={"ed": target}, device_id_type=MESH,
        )

    def peer(d):
        return lax.rem(me + d, n_ep)

    spans = [pl.ds(2 * a * LANES, 2 * LANES) for a in range(whole)] + [pl.ds(lead, rest)]

    def row_copy(i, a, d, src):
        return to_ep(
            outrows.at[i, peer(d), :, spans[a]], rows.at[i, src, :, spans[a]],
            row_ss.at[i, a, d], row_rs.at[i, a, src], d,
        )

    def gate_copy(d, src):
        return to_ep(gate_out.at[peer(d)], gate_in.at[src], gate_ss.at[d], gate_rs.at[src], d)

    def score_copy(d, src):
        return to_ep(score_out.at[peer(d)], score_in.at[src], score_ss.at[d], score_rs.at[src], d)

    def hist_copy(d, src):
        return to_ed(
            hist_mine, hist_all.at[src], hist_ss.at[d], hist_rs.at[src], lax.rem(ed + d, n_ed)
        )

    def amax_copy(d, src):
        return to_ed(
            amax_mine, amax_all.at[src], amax_ss.at[d], amax_rs.at[src], lax.rem(ed + d, n_ed)
        )

    def dispatch(i, a):
        for d in range(1, n_ep):
            row_copy(i, a, d, me).start()

    for d in range(1, n_ep):
        gate_copy(d, me).start()
    dispatch(0, 0)

    tile = 32
    pre_in.wait()
    for d in range(1, n_ep):
        gate_copy(d, peer(d)).wait_recv()

    @pl.loop(0, slots // tile)
    def _(t):
        at = pl.ds(pl.multiple_of(t * tile, tile), tile)
        src, off = t // (cap // tile), t % (cap // tile)
        off = pl.multiple_of(off * tile, tile)
        g = pre[src, pl.ds(off, tile), 0:ff].astype(f32)
        u = pre[src, pl.ds(off, tile), ff:].astype(f32)
        a = (g * jax.nn.sigmoid(g) * u).astype(bf16)
        act[at, :] = a
        gate = gate_in[src, pl.ds(off, tile), 0:1].astype(f32)
        w2[core, at, :] = (gate * a.astype(f32)).astype(bf16)

    def w2_copy(which):
        return to_ed(w2.at[which], w2.at[which], w2_ss.at[0], w2_rs.at[0], sibling)

    w2_copy(core).start()
    for d in range(1, n_ed):
        hist_copy(d, ed).start()
    hist_all[ed] = hist_mine[...]
    place_rows(1)

    def window(a, which):
        if a < whole:
            return pl.ds(pl.multiple_of((2 * a + which) * LANES, LANES), LANES)
        return pl.ds(pl.multiple_of(lead + which * (rest - win), LANES), win)

    heights = [LANES] * whole + [small]
    starts = [a * LANES for a in range(parts)]
    wide = [LANES] * whole + [win]

    def sib_copy(i, a):
        return to_ed(
            rows.at[i, :, :, window(a, 1 - core)], sib.at[i, a, :, :, pl.ds(0, wide[a])],
            sib_ss.at[i, a], sib_rs.at[i, a], sibling,
        )

    def direction(i):
        ahead = lax.rem(shard[i] - z + n_z, n_z)
        right = jnp.where(2 * ahead == n_z, shard[i] > z, 2 * ahead < n_z)
        before = lax.rem(shard[i] - z + 1 + n_z, n_z)
        fed_right = jnp.logical_and(2 * before == n_z, jnp.logical_and(z > 0, shard[i] > z))
        behind = lax.rem(z + 1 - shard[i] + n_z, n_z)
        fed_left = jnp.logical_and(2 * behind == n_z, jnp.logical_and(z < n_z - 1, shard[i] < z))
        return right, jnp.where(right, fed_right, fed_left)

    def z_copy(i, s):
        right, _ = direction(i)
        target = lax.rem(jnp.where(right, z + 1, z + n_z - 1), n_z)
        way = jnp.where(right, 0, 1)
        at = pl.ds(starts[s], heights[s])
        return to_ed(
            zsend.at[i, at], recv.at[way, shard[i], at], z_ss.at[i, s],
            z_rs.at[way, shard[i], s], target * 2 + core,
        )

    def z_arrival(way, j, s):
        at = pl.ds(starts[s], heights[s])
        return to_ed(
            zsend.at[0, at], recv.at[way, j, at], z_ss.at[0, 0], z_rs.at[way, j, s], sibling
        )

    n_tile = 256
    etile = 32

    def part(i, a):
        sib_copy(i, a).start()
        rt[0 : wide[a], pl.ds(pl.multiple_of(core * slots, LANES), slots)] = (
            rows[i, :, :, window(a, core)].reshape(slots, wide[a]).T
        )
        if i == 0 and a == 0:
            w2_copy(1 - core).wait_recv()
        sib_copy(i, a).wait_recv()
        rt[0 : wide[a], pl.ds(pl.multiple_of((1 - core) * slots, LANES), slots)] = (
            sib[i, a, :, :, 0 : wide[a]].reshape(slots, wide[a]).T
        )
        skip = 0 if a < whole else pl.multiple_of((small - (rest - win)) * core, 16)

        @pl.loop(0, ff // n_tile)
        def _(n):
            at = pl.ds(pl.multiple_of(n * n_tile, n_tile), n_tile)
            acc[starts[a] : starts[a] + heights[a], at] = jnp.dot(
                rt[pl.ds(skip, heights[a]), :],
                w2[:, :, at].reshape(2 * slots, n_tile),
                preferred_element_type=f32,
            )

    def send_on(i, s, came_by):
        @pl.loop(0, heights[s] // etile)
        def _(t):
            at = pl.ds(pl.multiple_of(starts[s] + t * etile, etile), etile)
            value = acc[at, :]
            if came_by is not None:
                value = value + recv[came_by, shard[i], at, :].astype(f32)
            zsend[i, at, :] = value.astype(bf16)

        if i > 0:
            z_copy(i - 1, s).wait_send()
        z_copy(i, s).start()

    for i in range(n_z):
        last = i == n_z - 1
        right, fed = direction(i)
        way = jnp.where(right, 0, 1)
        for a in range(parts):
            for d in range(1, n_ep):
                row_copy(i, a, d, peer(d)).wait_recv()
            if i == 0 and a + 1 < parts:
                dispatch(0, a + 1)
            if not last and a == parts - 1:
                for nxt in range(parts):
                    dispatch(i + 1, nxt)
            part(i, a)
            if not last:

                @pl.when(jnp.logical_not(fed))
                def _():
                    send_on(i, a, None)

        for copy in w_in[i]:
            copy.wait()

        @pl.loop(0, ff // n_tile)
        def _(n):
            at = pl.ds(pl.multiple_of(n * n_tile, n_tile), n_tile)
            got = lax.dot_general(
                rows[i].reshape(slots, blk), wv[i, at, :], (((1,), (1,)), ((), ())),
                preferred_element_type=f32,
            )
            if i == 0:
                raw[:, at] = got
            else:
                raw[:, at] += got

        if i + 2 < n_z:
            place_rows(i + 2)
        if last:
            break

        @pl.when(fed)
        def _():
            for s in range(parts):
                z_arrival(way, shard[i], s).wait_recv()
                send_on(i, s, way)

    @pl.loop(0, slots // tile)
    def _(t):
        at = pl.ds(pl.multiple_of(t * tile, tile), tile)
        src, off = t // (cap // tile), t % (cap // tile)
        off = pl.multiple_of(off * tile, tile)
        g = pre[src, pl.ds(off, tile), 0:ff].astype(f32)
        u = pre[src, pl.ds(off, tile), ff:].astype(f32)
        sigma = jax.nn.sigmoid(g)
        r = raw[at, :]
        total = jnp.sum(act[at, :].astype(f32) * r, axis=1, keepdims=True)
        score_out[src, pl.ds(off, tile), :] = jnp.broadcast_to(total, (tile, LANES))
        gr = gate_in[src, pl.ds(off, tile), 0:1].astype(f32) * r
        pgrad[src, pl.ds(off, tile), 0:ff] = (gr * u * sigma * (1.0 + g * (1.0 - sigma))).astype(
            bf16
        )
        pgrad[src, pl.ds(off, tile), ff:] = (gr * g * sigma).astype(bf16)

    for d in range(1, n_ep):
        score_copy(d, me).start()
    score_in[me] = score_out[me]

    for d in range(1, n_ed):
        hist_copy(d, lax.rem(ed + d, n_ed)).wait_recv()
    merged = jnp.max(hist_all[...], axis=0)
    ref_amax = jnp.max(merged)
    scale = 1.0 / jnp.full((1, 1), ref_amax, f32)

    for d in range(1, n_ep):
        score_copy(d, peer(d)).wait_recv()
    value0 = jnp.zeros((1, tokens), f32)
    value1 = jnp.zeros((1, tokens), f32)
    for e in range(n_ep):
        found = jnp.sum(perm_t[e] * score_in[e], axis=0, keepdims=True)
        value0 = value0 + jnp.where(first == e, found, 0.0)
        value1 = value1 + jnp.where(second == e, found, 0.0)
    gg_out[0:1, :] = value0
    gg_out[1:2, :] = value1

    amax_mine[...] = jnp.zeros_like(amax_mine)
    for s in range(parts):
        for way in range(2):
            z_arrival(way, z, s).wait_recv()
        base = jnp.where(core == 0, starts[s], half - starts[s] - heights[s])

        @pl.loop(0, heights[s] // etile)
        def _(t):
            at = pl.ds(pl.multiple_of(starts[s] + t * etile, etile), etile)
            came = recv[0, z, at, :].astype(f32) + recv[1, z, at, :].astype(f32)
            value = (acc[at, :] + came) * scale
            wg_out[0, pl.ds(pl.multiple_of(base + t * etile, etile), etile), :] = value
            large = jnp.max(jnp.abs(value).reshape(etile // 8, 8, ff // LANES, LANES), axis=(0, 2))
            amax_mine[...] = jnp.maximum(amax_mine[...], large)

    for d in range(1, n_ed):
        amax_copy(d, ed).start()
    amax_all[ed] = amax_mine[...]
    for d in range(1, n_ed):
        amax_copy(d, lax.rem(ed + d, n_ed)).wait_recv()
    peak = jnp.max(amax_all[...]) * ref_amax
    width = hist_ref.shape[1]
    moved = pltpu.roll(merged, LANES - 1, 1)
    lane = lax.broadcasted_iota(jnp.int32, merged.shape, 1)
    hist_out[...] = jnp.where(lane == width - 1, peak, moved)[0:1, 0:width]

    for d in range(1, n_ep):
        for i in range(n_z):
            for a in range(parts):
                row_copy(i, a, d, me).wait_send()
        gate_copy(d, me).wait_send()
        score_copy(d, me).wait_send()
    for d in range(1, n_ed):
        hist_copy(d, ed).wait_send()
        amax_copy(d, ed).wait_send()
    w2_copy(core).wait_send()
    for i in range(n_z):
        for a in range(parts):
            sib_copy(i, a).wait_send()
    for s in range(parts):
        z_copy(n_z - 2, s).wait_send()


def fused(out_grad, routes, gates, pre_acts, down_weight, history):
    f32, bf16, dma = jnp.float32, jnp.bfloat16, pltpu.SemaphoreType.DMA
    tokens, width = out_grad.shape
    ff = down_weight.shape[1]
    n_src, cap = pre_acts.shape[2], pre_acts.shape[3]
    n_ep, n_ed = lax.axis_size("ep"), lax.axis_size("ed")
    n_z = n_ed // 2
    hist = history.shape[2]
    blk = width // n_z
    half = blk // 2
    whole, small, win = split_half(half)
    parts, lead = whole + 1, max(LANES, win)
    slots = n_ep * cap
    vmem, anywhere = pl.BlockSpec(memory_space=pltpu.VMEM), pl.BlockSpec(memory_space=pl.ANY)
    pre_grad, wgrad, new_history, gate_grad = pl.pallas_call(
        functools.partial(kernel, n_z, n_ep, cap),
        out_shape=(
            pltpu.VMEM((n_src, cap, 2 * ff), bf16),
            pltpu.VMEM((1, half, ff), f32),
            jax.ShapeDtypeStruct((1, hist), f32),
            jax.ShapeDtypeStruct((2, tokens), f32),
        ),
        in_specs=[vmem, vmem, vmem, anywhere, anywhere, anywhere],
        out_specs=(vmem, vmem, vmem, vmem),
        scratch_shapes=[
            pltpu.VMEM((n_z, tokens, blk), bf16),
            pltpu.VMEM((n_z, ff, blk), bf16),
            pltpu.VMEM((n_src, cap, 2 * ff), bf16),
            pltpu.VMEM((n_ep, cap, tokens), bf16),
            pltpu.VMEM((n_ep, cap, tokens), f32),
            pltpu.VMEM((n_z, n_ep, cap, blk), bf16),
            pltpu.VMEM((n_z, n_ep, cap, blk), bf16),
            pltpu.VMEM((n_z, parts, n_ep, cap, lead), bf16),
            pltpu.VMEM((2, slots, ff), bf16),
            pltpu.VMEM((slots, ff), f32),
            pltpu.VMEM((slots, ff), bf16),
            pltpu.VMEM((lead, 2 * slots), bf16),
            pltpu.VMEM((half, ff), f32),
            pltpu.VMEM((2, n_z, half, ff), bf16),
            pltpu.VMEM((n_z - 1, half, ff), bf16),
            pltpu.VMEM((n_ep, cap, LANES), bf16),
            pltpu.VMEM((n_ep, cap, LANES), bf16),
            pltpu.VMEM((n_ep, cap, LANES), f32),
            pltpu.VMEM((n_ep, cap, LANES), f32),
            pltpu.VMEM((8, LANES), f32),
            pltpu.VMEM((n_ed, 8, LANES), f32),
            pltpu.VMEM((8, LANES), f32),
            pltpu.VMEM((n_ed, 8, LANES), f32),
            dma((n_z, 2 * whole + 1)),
            dma((n_z, 2 * whole + 1)),
            dma((1,)),
            dma((n_z, parts, n_ep)),
            dma((n_z, parts, n_ep)),
            dma((n_ep,)),
            dma((n_ep,)),
            dma((n_ep,)),
            dma((n_ep,)),
            dma((n_z, parts)),
            dma((n_z, parts)),
            dma((1,)),
            dma((1,)),
            dma((n_z, parts)),
            dma((2, n_z, parts)),
            dma((n_ed,)),
            dma((n_ed,)),
            dma((n_ed,)),
            dma((n_ed,)),
        ],
        compiler_params=pltpu.CompilerParams(
            collective_id=0, has_side_effects=True, vmem_limit_bytes=56 * 1024 * 1024
        ),
        cost_estimate=pl.CostEstimate(
            flops=4 * slots * width * ff, bytes_accessed=16 * 1024 * 1024, transcendentals=slots * ff
        ),
    )(
        routes.T, gates.T, history[0], out_grad, pre_acts[0, 0], down_weight
    )
    return pre_grad[None, None], wgrad, new_history, gate_grad.T


def body(out_grad, routes, gates, pre_acts, down_weight, history):
    tokens, width = out_grad.shape
    cap = pre_acts.shape[3]
    n_ed = lax.axis_size("ed")
    fits = (
        n_ed % 2 == 0
        and n_ed == 8
        and cap == LANES
        and tokens == LANES
        and down_weight.shape[0] == 1
        and width % (n_ed // 2 * LANES) == 0
        and width // n_ed % 64 == 0
        and lax.axis_size("ep") <= 16
    )
    run = fused if fits else plain
    return run(out_grad, routes, gates, pre_acts, down_weight, history)


def solution(mesh):
    placed = (
        P(("ed", "ep"), None),
        P(("ed", "ep"), None),
        P(("ed", "ep"), None),
        P("ed", "ep", None, None, None),
        P("ep", None, None),
        P("ed", "ep", None),
    )
    return jax.shard_map(
        body,
        mesh=mesh,
        in_specs=placed,
        out_specs=(
            P("ed", "ep", None, None, None),
            P("ep", "ed", None),
            P("ep", None),
            P(("ed", "ep"), None),
        ),
        check_vma=False,
    )
```

```python
import functools

import jax
import jax.numpy as jnp
from jax import lax
from jax.experimental import pallas as pl
from jax.experimental.pallas import tpu as pltpu
from jax.sharding import PartitionSpec as P


def split_pre(pre_block, width_ff):
    gate_pre = pre_block[:, :width_ff].astype(jnp.float32)
    up_pre = pre_block[:, width_ff:].astype(jnp.float32)
    return (gate_pre, up_pre, jax.nn.sigmoid(gate_pre))


def plain(out_grad, routes, gates, pre_acts, down_weight, history):
    tok_rows, top = routes.shape
    width = out_grad.shape[1]
    local = down_weight.shape[0]
    width_ff = down_weight.shape[1]
    n_src = pre_acts.shape[2]
    cap = pre_acts.shape[3]
    n_ep = lax.axis_size("ep")
    n_replicas = lax.axis_size("ed")
    experts = local * n_ep
    flat = routes.reshape(-1)
    hits = (flat[:, None] == jnp.arange(experts, dtype=jnp.int32)[None, :]).astype(jnp.int32)
    before = jnp.cumsum(hits, axis=0) - hits
    slot = jnp.sum(before * hits, axis=1)
    target = flat * cap + slot
    owner = jnp.arange(tok_rows * top, dtype=jnp.int32) // top
    table = jnp.zeros((experts * cap,), jnp.int32).at[target].set(owner + 1)
    picked = out_grad[jnp.maximum(table - 1, 0)]
    send_rows = jnp.where((table > 0)[:, None], picked, jnp.zeros_like(picked))
    send_gate = jnp.zeros((experts * cap,), jnp.bfloat16).at[target].set(gates.reshape(-1))
    arrived, arrived_gate = (
        lax.all_to_all(
            send_rows.reshape(n_ep, local * cap, width),
            "ep",
            split_axis=0,
            concat_axis=0,
            tiled=True,
        ),
        lax.all_to_all(
            send_gate.reshape(n_ep, local * cap), "ep", split_axis=0, concat_axis=0, tiled=True
        ),
    )
    arrived = (
        arrived.reshape(n_ep, local, cap, width)
        .transpose(1, 0, 2, 3)
        .reshape(local, n_ep * cap, width)
    )
    arrived_gate = (
        arrived_gate.reshape(n_ep, local, cap)
        .transpose(1, 0, 2)
        .reshape(local, n_ep * cap)
        .astype(jnp.float32)
    )
    merged = lax.pmax(history, "ed")[0]
    ref_amax = jnp.max(merged, axis=1)
    scale = 1.0 / ref_amax
    rows = arrived[0]
    gate_row = arrived_gate[0][:, None]
    weight = down_weight[0]
    pre_block = pre_acts[0, 0].reshape(n_src * cap, 2 * width_ff)
    gate_pre, up_pre, sigma = split_pre(pre_block, width_ff)
    act = (gate_pre * sigma * up_pre).astype(jnp.bfloat16)
    weighted = (gate_row * act.astype(jnp.float32)).astype(jnp.bfloat16)
    raw = jnp.einsum("rd,hd->rh", rows, weight, preferred_element_type=jnp.float32)
    score = jnp.sum(act.astype(jnp.float32) * raw, axis=1)
    grad_act = gate_row * raw
    grad_gate = grad_act * up_pre * sigma * (1.0 + gate_pre * (1.0 - sigma))
    grad_up = grad_act * gate_pre * sigma
    grads_pre = [
        jnp.concatenate([grad_gate, grad_up], axis=1)
        .astype(jnp.bfloat16)
        .reshape(n_src, cap, 2 * width_ff)
    ]
    scores = [score.reshape(n_ep, cap)]
    factor = scale[0]

    def term(start, count, rows=rows, weighted=weighted, factor=factor):
        return factor * jnp.einsum("rd,rh->dh", rows, weighted, preferred_element_type=jnp.float32)

    shard = lax.psum_scatter(
        term(jnp.int32(0), width // n_replicas * lax.axis_size("ed")).astype(jnp.bfloat16),
        "ed",
        scatter_dimension=0,
        tiled=True,
    ).astype(jnp.float32)
    shards = [shard]
    wgrad = jnp.stack(shards)
    peak = lax.pmax(jnp.max(jnp.abs(wgrad), axis=(1, 2)), "ed")
    new_amax = peak * ref_amax
    new_history = jnp.concatenate([merged[:, 1:], new_amax[:, None]], axis=1)
    pre_grad = jnp.stack(grads_pre)[None]
    outgoing = jnp.stack(scores).transpose(1, 0, 2).reshape(n_ep, local * cap)
    returned = lax.all_to_all(outgoing, "ep", split_axis=0, concat_axis=0, tiled=True)
    gate_grad = returned.reshape(-1)[target].reshape(tok_rows, top)
    return (pre_grad, wgrad, new_history, gate_grad)


MESH = pl.DeviceIdType.MESH
LANES = 128


def orders(n_z):
    centre = (n_z - 1) / 2
    return [
        sorted(range(n_z), key=lambda j: (-abs(j - z), -abs(j - centre), j)) for z in range(n_z)
    ]


def split_half(half):
    whole = max(half // LANES - 1, 0)
    small = half - whole * LANES
    return whole, small, -(-small // LANES) * LANES


def kernel(
    n_z,
    n_ep,
    cap,
    routes_ref,
    gates_ref,
    hist_ref,
    tok_hbm,
    pre_hbm,
    w_hbm,
    pgrad,
    wg_out,
    hist_out,
    gg_out,
    tok,
    wv,
    pre,
    perm,
    perm_t,
    outrows,
    rows,
    sib,
    w2,
    raw,
    act,
    rt,
    acc,
    recv,
    zsend,
    gate_out,
    gate_in,
    score_out,
    score_in,
    hist_mine,
    hist_all,
    amax_mine,
    amax_all,
    tok_sem,
    w_sem,
    pre_sem,
    row_ss,
    row_rs,
    gate_ss,
    gate_rs,
    score_ss,
    score_rs,
    sib_ss,
    sib_rs,
    w2_ss,
    w2_rs,
    z_ss,
    z_rs,
    hist_ss,
    hist_rs,
    amax_ss,
    amax_rs,
):
    f32, bf16 = jnp.float32, jnp.bfloat16
    ed, me = lax.axis_index("ed"), lax.axis_index("ep")
    z, core = ed // 2, ed % 2
    n_ed = 2 * n_z
    sibling = z * 2 + 1 - core
    blk = tok.shape[2]
    half = blk // 2
    whole, small, win = split_half(half)
    parts = whole + 1
    lead = 2 * whole * LANES
    rest = blk - lead
    slots = n_ep * cap
    ff = act.shape[1]
    table = orders(n_z)

    def shard_at(i):
        j = jnp.int32(table[0][i])
        for at in range(1, n_z):
            j = jnp.where(z == at, jnp.int32(table[at][i]), j)
        return j

    shard = [shard_at(i) for i in range(n_z)]

    pieces = []
    for a in range(whole):
        pieces.append((a * LANES, 2 * a * LANES, LANES))
        pieces.append((blk - (a + 1) * LANES, (2 * a + 1) * LANES, LANES))
    pieces.append((whole * LANES, lead, rest))

    def columns(i, begin, count):
        return pl.ds(pl.multiple_of(shard[i] * blk + begin, LANES), count)

    tok_in = [
        [
            pltpu.make_async_copy(
                tok_hbm.at[:, columns(i, begin, count)],
                tok.at[i, :, pl.ds(to, count)],
                tok_sem.at[i, p],
            )
            for p, (begin, to, count) in enumerate(pieces)
        ]
        for i in range(n_z)
    ]
    w_in = [
        [
            pltpu.make_async_copy(
                w_hbm.at[0, :, columns(i, begin, count)],
                wv.at[i, :, pl.ds(to, count)],
                w_sem.at[i, p],
            )
            for p, (begin, to, count) in enumerate(pieces)
        ]
        for i in range(n_z)
    ]
    pre_in = pltpu.make_async_copy(pre_hbm, pre, pre_sem.at[0])
    for copy in tok_in[0]:
        copy.start()
    pre_in.start()
    for i in range(1, n_z):
        for copy in tok_in[i]:
            copy.start()
    for i in range(n_z):
        for copy in w_in[i]:
            copy.start()

    barrier = pltpu.get_barrier_semaphore()
    for d in range(1, n_ep):
        pl.semaphore_signal(
            barrier, inc=1, device_id={"ep": lax.rem(me + d, n_ep)}, device_id_type=MESH
        )
    for d in range(1, n_ed):
        pl.semaphore_signal(
            barrier, inc=1, device_id={"ed": lax.rem(ed + d, n_ed)}, device_id_type=MESH
        )

    hist_mine[...] = jnp.zeros_like(hist_mine)
    hist_mine[0:1, 0 : hist_ref.shape[1]] = hist_ref[...]

    tokens = tok.shape[1]
    first, second = routes_ref[0:1, :], routes_ref[1:2, :]
    gate0, gate1 = gates_ref[0:1, :].astype(f32), gates_ref[1:2, :].astype(f32)
    expert = lax.broadcasted_iota(jnp.int32, (16, tokens), 0)
    hits = jnp.where(first == expert, 1.0, 0.0) + jnp.where(second == expert, 1.0, 0.0)
    earlier = lax.broadcasted_iota(jnp.int32, (tokens, tokens), 0) < lax.broadcasted_iota(
        jnp.int32, (tokens, tokens), 1
    )
    slot = jnp.dot(
        hits.astype(bf16), jnp.where(earlier, 1.0, 0.0).astype(bf16), preferred_element_type=f32
    )
    place = lax.broadcasted_iota(jnp.int32, (cap, tokens), 0).astype(f32)
    for e in range(n_ep):
        own = jnp.where(slot[e : e + 1, :] == place, hits[e : e + 1, :], 0.0)
        perm_t[e] = own
        perm[e] = own.astype(bf16)
        gate = jnp.where(first == e, gate0, 0.0) + jnp.where(second == e, gate1, 0.0)
        column = jnp.sum(own * gate, axis=1, keepdims=True)
        gate_out[e] = jnp.broadcast_to(column, (cap, LANES)).astype(bf16)
    gate_in[me] = gate_out[me]

    def place_rows(i):
        for copy in tok_in[i]:
            copy.wait()

        @pl.loop(0, n_ep)
        def _(e):
            outrows[i, e] = jnp.dot(perm[e], tok[i], preferred_element_type=f32).astype(bf16)

        rows[i, me] = outrows[i, me]

    place_rows(0)
    pl.semaphore_wait(barrier, n_ep - 1 + n_ed - 1)

    def to_ep(src, dst, ss, rs, d):
        return pltpu.make_async_remote_copy(
            src_ref=src, dst_ref=dst, send_sem=ss, recv_sem=rs,
            device_id={"ep": lax.rem(me + d, n_ep)}, device_id_type=MESH,
        )

    def to_ed(src, dst, ss, rs, target):
        return pltpu.make_async_remote_copy(
            src_ref=src, dst_ref=dst, send_sem=ss, recv_sem=rs,
            device_id={"ed": target}, device_id_type=MESH,
        )

    def peer(d):
        return lax.rem(me + d, n_ep)

    spans = [pl.ds(2 * a * LANES, 2 * LANES) for a in range(whole)] + [pl.ds(lead, rest)]

    def row_copy(i, a, d, src):
        return to_ep(
            outrows.at[i, peer(d), :, spans[a]], rows.at[i, src, :, spans[a]],
            row_ss.at[i, a, d], row_rs.at[i, a, src], d,
        )

    def gate_copy(d, src):
        return to_ep(gate_out.at[peer(d)], gate_in.at[src], gate_ss.at[d], gate_rs.at[src], d)

    def score_copy(d, src):
        return to_ep(score_out.at[peer(d)], score_in.at[src], score_ss.at[d], score_rs.at[src], d)

    def hist_copy(d, src):
        return to_ed(
            hist_mine, hist_all.at[src], hist_ss.at[d], hist_rs.at[src], lax.rem(ed + d, n_ed)
        )

    def amax_copy(d, src):
        return to_ed(
            amax_mine, amax_all.at[src], amax_ss.at[d], amax_rs.at[src], lax.rem(ed + d, n_ed)
        )

    def dispatch(i, a):
        for d in range(1, n_ep):
            row_copy(i, a, d, me).start()

    for d in range(1, n_ep):
        gate_copy(d, me).start()
    dispatch(0, 0)

    tile = 32
    pre_in.wait()
    for d in range(1, n_ep):
        gate_copy(d, peer(d)).wait_recv()

    @pl.loop(0, slots // tile)
    def _(t):
        at = pl.ds(pl.multiple_of(t * tile, tile), tile)
        src, off = t // (cap // tile), t % (cap // tile)
        off = pl.multiple_of(off * tile, tile)
        g = pre[src, pl.ds(off, tile), 0:ff].astype(f32)
        u = pre[src, pl.ds(off, tile), ff:].astype(f32)
        a = (g * jax.nn.sigmoid(g) * u).astype(bf16)
        act[at, :] = a
        gate = gate_in[src, pl.ds(off, tile), 0:1].astype(f32)
        w2[core, at, :] = (gate * a.astype(f32)).astype(bf16)

    def w2_copy(which):
        return to_ed(w2.at[which], w2.at[which], w2_ss.at[0], w2_rs.at[0], sibling)

    w2_copy(core).start()
    for d in range(1, n_ed):
        hist_copy(d, ed).start()
    hist_all[ed] = hist_mine[...]
    place_rows(1)

    @pl.when(z == 0)
    def _():
        recv[0, z] = jnp.zeros(recv.shape[2:], bf16)

    @pl.when(z == n_z - 1)
    def _():
        recv[1, z] = jnp.zeros(recv.shape[2:], bf16)

    def window(a, which):
        if a < whole:
            return pl.ds(pl.multiple_of((2 * a + which) * LANES, LANES), LANES)
        return pl.ds(pl.multiple_of(lead + which * (rest - win), LANES), win)

    heights = [LANES] * whole + [small]
    starts = [a * LANES for a in range(parts)]
    wide = [LANES] * whole + [win]

    def sib_copy(i, a):
        return to_ed(
            rows.at[i, :, :, window(a, 1 - core)], sib.at[i, a, :, :, pl.ds(0, wide[a])],
            sib_ss.at[i, a], sib_rs.at[i, a], sibling,
        )

    def direction(i):
        right = shard[i] > z
        return right, jnp.where(right, z > 0, z < n_z - 1)

    def z_copy(i, s):
        right, _ = direction(i)
        target = jnp.where(right, z + 1, z - 1)
        way = jnp.where(right, 0, 1)
        at = pl.ds(starts[s], heights[s])
        return to_ed(
            zsend.at[i, at], recv.at[way, shard[i], at], z_ss.at[i, s],
            z_rs.at[way, shard[i], s], target * 2 + core,
        )

    def z_arrival(way, j, s):
        at = pl.ds(starts[s], heights[s])
        return to_ed(
            zsend.at[0, at], recv.at[way, j, at], z_ss.at[0, 0], z_rs.at[way, j, s], sibling
        )

    n_tile = 256
    etile = 32

    def part(i, a):
        sib_copy(i, a).start()
        rt[0 : wide[a], pl.ds(pl.multiple_of(core * slots, LANES), slots)] = (
            rows[i, :, :, window(a, core)].reshape(slots, wide[a]).T
        )
        if i == 0 and a == 0:
            w2_copy(1 - core).wait_recv()
        sib_copy(i, a).wait_recv()
        rt[0 : wide[a], pl.ds(pl.multiple_of((1 - core) * slots, LANES), slots)] = (
            sib[i, a, :, :, 0 : wide[a]].reshape(slots, wide[a]).T
        )
        skip = 0 if a < whole else pl.multiple_of((small - (rest - win)) * core, 16)

        @pl.loop(0, ff // n_tile)
        def _(n):
            at = pl.ds(pl.multiple_of(n * n_tile, n_tile), n_tile)
            acc[starts[a] : starts[a] + heights[a], at] = jnp.dot(
                rt[pl.ds(skip, heights[a]), :],
                w2[:, :, at].reshape(2 * slots, n_tile),
                preferred_element_type=f32,
            )

    def send_on(i, s, came_by):
        @pl.loop(0, heights[s] // etile)
        def _(t):
            at = pl.ds(pl.multiple_of(starts[s] + t * etile, etile), etile)
            value = acc[at, :]
            if came_by is not None:
                value = value + recv[came_by, shard[i], at, :].astype(f32)
            zsend[i, at, :] = value.astype(bf16)

        if i > 0:
            z_copy(i - 1, s).wait_send()
        z_copy(i, s).start()

    for i in range(n_z):
        last = i == n_z - 1
        right, fed = direction(i)
        way = jnp.where(right, 0, 1)
        for a in range(parts):
            for d in range(1, n_ep):
                row_copy(i, a, d, peer(d)).wait_recv()
            if i == 0 and a + 1 < parts:
                dispatch(0, a + 1)
            if not last and a == parts - 1:
                for nxt in range(parts):
                    dispatch(i + 1, nxt)
            part(i, a)
            if not last:

                @pl.when(jnp.logical_not(fed))
                def _():
                    send_on(i, a, None)

        for copy in w_in[i]:
            copy.wait()

        @pl.loop(0, ff // n_tile)
        def _(n):
            at = pl.ds(pl.multiple_of(n * n_tile, n_tile), n_tile)
            got = lax.dot_general(
                rows[i].reshape(slots, blk), wv[i, at, :], (((1,), (1,)), ((), ())),
                preferred_element_type=f32,
            )
            if i == 0:
                raw[:, at] = got
            else:
                raw[:, at] += got

        if i + 2 < n_z:
            place_rows(i + 2)
        if last:
            break

        @pl.when(fed)
        def _():
            for s in range(parts):
                z_arrival(way, shard[i], s).wait_recv()
                send_on(i, s, way)

    @pl.loop(0, slots // tile)
    def _(t):
        at = pl.ds(pl.multiple_of(t * tile, tile), tile)
        src, off = t // (cap // tile), t % (cap // tile)
        off = pl.multiple_of(off * tile, tile)
        g = pre[src, pl.ds(off, tile), 0:ff].astype(f32)
        u = pre[src, pl.ds(off, tile), ff:].astype(f32)
        sigma = jax.nn.sigmoid(g)
        r = raw[at, :]
        total = jnp.sum(act[at, :].astype(f32) * r, axis=1, keepdims=True)
        score_out[src, pl.ds(off, tile), :] = jnp.broadcast_to(total, (tile, LANES))
        gr = gate_in[src, pl.ds(off, tile), 0:1].astype(f32) * r
        pgrad[src, pl.ds(off, tile), 0:ff] = (gr * u * sigma * (1.0 + g * (1.0 - sigma))).astype(
            bf16
        )
        pgrad[src, pl.ds(off, tile), ff:] = (gr * g * sigma).astype(bf16)

    for d in range(1, n_ep):
        score_copy(d, me).start()
    score_in[me] = score_out[me]

    for d in range(1, n_ed):
        hist_copy(d, lax.rem(ed + d, n_ed)).wait_recv()
    merged = jnp.max(hist_all[...], axis=0)
    ref_amax = jnp.max(merged)
    scale = 1.0 / jnp.full((1, 1), ref_amax, f32)

    for d in range(1, n_ep):
        score_copy(d, peer(d)).wait_recv()
    value0 = jnp.zeros((1, tokens), f32)
    value1 = jnp.zeros((1, tokens), f32)
    for e in range(n_ep):
        found = jnp.sum(perm_t[e] * score_in[e], axis=0, keepdims=True)
        value0 = value0 + jnp.where(first == e, found, 0.0)
        value1 = value1 + jnp.where(second == e, found, 0.0)
    gg_out[0:1, :] = value0
    gg_out[1:2, :] = value1

    amax_mine[...] = jnp.zeros_like(amax_mine)
    for s in range(parts):

        @pl.when(z > 0)
        def _():
            z_arrival(0, z, s).wait_recv()

        @pl.when(z < n_z - 1)
        def _():
            z_arrival(1, z, s).wait_recv()

        base = jnp.where(core == 0, starts[s], half - starts[s] - heights[s])

        @pl.loop(0, heights[s] // etile)
        def _(t):
            at = pl.ds(pl.multiple_of(starts[s] + t * etile, etile), etile)
            came = recv[0, z, at, :].astype(f32) + recv[1, z, at, :].astype(f32)
            value = (acc[at, :] + came) * scale
            wg_out[0, pl.ds(pl.multiple_of(base + t * etile, etile), etile), :] = value
            large = jnp.max(jnp.abs(value).reshape(etile // 8, 8, ff // LANES, LANES), axis=(0, 2))
            amax_mine[...] = jnp.maximum(amax_mine[...], large)

    for d in range(1, n_ed):
        amax_copy(d, ed).start()
    amax_all[ed] = amax_mine[...]
    for d in range(1, n_ed):
        amax_copy(d, lax.rem(ed + d, n_ed)).wait_recv()
    peak = jnp.max(amax_all[...]) * ref_amax
    width = hist_ref.shape[1]
    moved = pltpu.roll(merged, LANES - 1, 1)
    lane = lax.broadcasted_iota(jnp.int32, merged.shape, 1)
    hist_out[...] = jnp.where(lane == width - 1, peak, moved)[0:1, 0:width]

    for d in range(1, n_ep):
        for i in range(n_z):
            for a in range(parts):
                row_copy(i, a, d, me).wait_send()
        gate_copy(d, me).wait_send()
        score_copy(d, me).wait_send()
    for d in range(1, n_ed):
        hist_copy(d, ed).wait_send()
        amax_copy(d, ed).wait_send()
    w2_copy(core).wait_send()
    for i in range(n_z):
        for a in range(parts):
            sib_copy(i, a).wait_send()
    for s in range(parts):
        z_copy(n_z - 2, s).wait_send()


def fused(out_grad, routes, gates, pre_acts, down_weight, history):
    f32, bf16, dma = jnp.float32, jnp.bfloat16, pltpu.SemaphoreType.DMA
    tokens, width = out_grad.shape
    ff = down_weight.shape[1]
    n_src, cap = pre_acts.shape[2], pre_acts.shape[3]
    n_ep, n_ed = lax.axis_size("ep"), lax.axis_size("ed")
    n_z = n_ed // 2
    hist = history.shape[2]
    blk = width // n_z
    half = blk // 2
    whole, small, win = split_half(half)
    parts, lead = whole + 1, max(LANES, win)
    slots = n_ep * cap
    vmem, anywhere = pl.BlockSpec(memory_space=pltpu.VMEM), pl.BlockSpec(memory_space=pl.ANY)
    pre_grad, wgrad, new_history, gate_grad = pl.pallas_call(
        functools.partial(kernel, n_z, n_ep, cap),
        out_shape=(
            pltpu.VMEM((n_src, cap, 2 * ff), bf16),
            pltpu.VMEM((1, half, ff), f32),
            pltpu.VMEM((1, hist), f32),
            pltpu.VMEM((2, tokens), f32),
        ),
        in_specs=[vmem, vmem, vmem, anywhere, anywhere, anywhere],
        out_specs=(vmem, vmem, vmem, vmem),
        scratch_shapes=[
            pltpu.VMEM((n_z, tokens, blk), bf16),
            pltpu.VMEM((n_z, ff, blk), bf16),
            pltpu.VMEM((n_src, cap, 2 * ff), bf16),
            pltpu.VMEM((n_ep, cap, tokens), bf16),
            pltpu.VMEM((n_ep, cap, tokens), f32),
            pltpu.VMEM((n_z, n_ep, cap, blk), bf16),
            pltpu.VMEM((n_z, n_ep, cap, blk), bf16),
            pltpu.VMEM((n_z, parts, n_ep, cap, lead), bf16),
            pltpu.VMEM((2, slots, ff), bf16),
            pltpu.VMEM((slots, ff), f32),
            pltpu.VMEM((slots, ff), bf16),
            pltpu.VMEM((lead, 2 * slots), bf16),
            pltpu.VMEM((half, ff), f32),
            pltpu.VMEM((2, n_z, half, ff), bf16),
            pltpu.VMEM((n_z - 1, half, ff), bf16),
            pltpu.VMEM((n_ep, cap, LANES), bf16),
            pltpu.VMEM((n_ep, cap, LANES), bf16),
            pltpu.VMEM((n_ep, cap, LANES), f32),
            pltpu.VMEM((n_ep, cap, LANES), f32),
            pltpu.VMEM((8, LANES), f32),
            pltpu.VMEM((n_ed, 8, LANES), f32),
            pltpu.VMEM((8, LANES), f32),
            pltpu.VMEM((n_ed, 8, LANES), f32),
            dma((n_z, 2 * whole + 1)),
            dma((n_z, 2 * whole + 1)),
            dma((1,)),
            dma((n_z, parts, n_ep)),
            dma((n_z, parts, n_ep)),
            dma((n_ep,)),
            dma((n_ep,)),
            dma((n_ep,)),
            dma((n_ep,)),
            dma((n_z, parts)),
            dma((n_z, parts)),
            dma((1,)),
            dma((1,)),
            dma((n_z, parts)),
            dma((2, n_z, parts)),
            dma((n_ed,)),
            dma((n_ed,)),
            dma((n_ed,)),
            dma((n_ed,)),
        ],
        compiler_params=pltpu.CompilerParams(
            collective_id=0, has_side_effects=True, vmem_limit_bytes=56 * 1024 * 1024
        ),
        cost_estimate=pl.CostEstimate(
            flops=4 * slots * width * ff, bytes_accessed=16 * 1024 * 1024, transcendentals=slots * ff
        ),
    )(
        routes.T, gates.T, history[0], out_grad, pre_acts[0, 0], down_weight
    )
    return pre_grad[None, None], wgrad, new_history, gate_grad.T


def body(out_grad, routes, gates, pre_acts, down_weight, history):
    tokens, width = out_grad.shape
    cap = pre_acts.shape[3]
    n_ed = lax.axis_size("ed")
    fits = (
        n_ed % 2 == 0
        and n_ed > 2
        and cap == LANES
        and tokens == LANES
        and down_weight.shape[0] == 1
        and width % (n_ed // 2 * LANES) == 0
        and width // n_ed % 64 == 0
        and lax.axis_size("ep") <= 16
    )
    run = fused if fits else plain
    return run(out_grad, routes, gates, pre_acts, down_weight, history)


def solution(mesh):
    placed = (
        P(("ed", "ep"), None),
        P(("ed", "ep"), None),
        P(("ed", "ep"), None),
        P("ed", "ep", None, None, None),
        P("ep", None, None),
        P("ed", "ep", None),
    )
    return jax.shard_map(
        body,
        mesh=mesh,
        in_specs=placed,
        out_specs=(
            P("ed", "ep", None, None, None),
            P("ep", "ed", None),
            P("ep", None),
            P(("ed", "ep"), None),
        ),
        check_vma=False,
    )
```
